256 devices in a mesh: sx: 16 (over y, x), sy: 16 (over z, core).
Axes of the slice: x: 4, y: 4, z: 8, core: 2. Of those that a mesh axis runs over, the one named last changes fastest.
Arguments:
- dual_rhs: float32 [16, 32, 2, 384, 128], P('sx', 'sy'), may hold values from -6 to 6
- scaling: float32 [16, 32, 2, 384], P('sx', 'sy'), may hold values from 0.05 to 0.5
- dual_count: int32 [16, 32, 2], P('sx', 'sy'), may hold values from 1 to 384, as said below
- corner_map: int32 [16, 32, 4], P('sx', 'sy'), may hold values from 0 to 511, as said below
- local_ops: bfloat16 [16, 32, 1536, 1536], P('sx', 'sy'), as said below
- corner_basis: bfloat16 [16, 32, 12, 1536], P('sx', 'sy'), may hold values from -0.3125 to 0.3125
- coarse_inverse: float32 [1536, 1536], P('sx', 'sy'), as said below
Outputs:
- multipliers: float32 [16, 32, 2, 384, 128], P('sx', 'sy')
- residual: float32 [16, 32, 2, 384, 128], P('sx', 'sy')
The draws below stay inside these ranges and needn't reach their ends.
Inputs may be any that keep to these rules, and one draw needn't show every extreme that they name: Each edge uses its first dual_count rows; some edge uses all 384. `corner_map`: corner k of subdomain (i, j) is 0: +x+y, 1: -x+y, 2: +x-y, 3: -x-y; a corner shared by neighbouring subdomains has one node number, and every node is a corner of four subdomains. `local_ops`: each block is symmetric positive definite. `coarse_inverse`: symmetric positive definite.
All inputs are finite; a program needn't handle non-finite values.
Results may differ from the reference program's by a relative error of at most 0.017.
Values sent between devices are 32-bit elements; how exact they have to be, the bound alone decides.
No kernel may reach another device: no remote copies, remote signals or barrier semaphores. Data moves between devices by JAX's collectives and lax.ppermute only.
A program may use at most 64 MiB of HBM per device.

```python
import math
import jax
import jax.numpy as jnp
from jax import lax

NI = 1536
SIDE = 384
CS = 3
NRHS = 128
ITERS = 3
GX = 16
GY = 32
NODES = 512
NC = 1536


def symmetric_block(noise, diag_values):
    order = noise.shape[-1]
    mixed = (noise + jnp.swapaxes(noise, -1, -2)) * (0.5 / math.sqrt(order))
    identity = jnp.eye(order, dtype=jnp.float32)
    return mixed * (1.0 - identity) + identity * diag_values[..., None, :]


def draw_local_ops(key, part):
    key = jax.random.fold_in(key, 11)
    first, second = jax.random.split(key)
    noise = jax.random.normal(first, (GX, GY, NI, NI), jnp.float32)
    diag_values = jax.random.uniform(second, (GX, GY, NI), jnp.float32, 2.5, 5.0)
    return symmetric_block(noise, diag_values).astype(jnp.bfloat16)


def draw_coarse_inverse(key, part):
    key = jax.random.fold_in(key, 13)
    first, second = jax.random.split(key)
    noise = jax.random.normal(first, (NC, NC), jnp.float32)
    diag_values = jax.random.uniform(second, (NC,), jnp.float32, 2.5, 5.0)
    return symmetric_block(noise, diag_values)


def draw_dual_count(key, part):
    key = jax.random.fold_in(key, 17)
    counts = jax.random.randint(key, (GX, GY, 2), SIDE // 4, SIDE + 1, dtype=jnp.int32)
    return counts.at[0, 0, 0].set(SIDE)


def draw_corner_map(key, part):
    key = jax.random.fold_in(key, 23)
    number = jax.random.permutation(key, GX * GY).astype(jnp.int32).reshape(GX, GY)
    west_node = jnp.roll(number, 1, 0)
    south_node = jnp.roll(number, 1, 1)
    diagonal_node = jnp.roll(west_node, 1, 1)
    return jnp.stack([number, west_node, south_node, diagonal_node], -1)


def steps_of(rng, extent, shards, smallest, largest):
    def one(dim, parts):
        heights = jax.random.uniform(jax.random.fold_in(jax.random.fold_in(rng, 6), dim), (parts,), jnp.float32, smallest / len(shards), largest / len(shards))
        return jnp.repeat(jnp.exp(heights), extent[dim] // parts).reshape((-1,) + (1,) * (len(extent) - dim - 1))

    level = one(*shards[0])
    for cut in shards[1:]:
        level = level * one(*cut)
    return level


def centred(own_key, extent, width, limit, cuts=(), kind=jnp.bfloat16):
    values = jax.random.normal(own_key, extent, jnp.float32) * width
    if len(cuts) > 0:
        values = steps_of(own_key, extent, cuts, -0.22, 0.18) * values
    return jnp.clip(values, min=-limit, max=limit).astype(kind)


def setup_inputs(seed: int = 0) -> dict:
    key_of = jax.random.split(jax.random.key(seed), 8)
    dual_rhs = centred(key_of[0], (GX, GY, 2, SIDE, NRHS), 1.0, 6.0, ((0, 16), (1, 16)), jnp.float32)
    scaling = jnp.clip(jnp.exp(math.log(0.5) - 2.3025851 * jax.random.uniform(key_of[1], (GX, GY, 2, SIDE), jnp.float32) ** steps_of(key_of[1], (GX, GY, 2, SIDE), ((0, 16), (1, 16)), -0.2, 0.2)), 0.05, 0.5)
    dual_count = draw_dual_count(jax.random.fold_in(key_of[7], 71), 0)
    corner_map = draw_corner_map(jax.random.fold_in(key_of[7], 71), 0)
    local_ops = draw_local_ops(jax.random.fold_in(key_of[7], 71), 0)
    corner_basis = centred(key_of[5], (GX, GY, 4 * CS, NI), (NI // 4) ** -0.5, 0.3125, ((0, 16), (1, 16)))
    coarse_inverse = draw_coarse_inverse(jax.random.fold_in(key_of[7], 71), 0)
    return {"dual_rhs": dual_rhs, "scaling": scaling, "dual_count": dual_count, "corner_map": corner_map, "local_ops": local_ops, "corner_basis": corner_basis, "coarse_inverse": coarse_inverse}


def reference(dual_rhs, scaling, dual_count, corner_map, local_ops, corner_basis, coarse_inverse):
    highest = lax.Precision.HIGHEST
    active = (jnp.arange(SIDE, dtype=jnp.int32)[None, None, None, :] < dual_count[..., None]).astype(jnp.float32)[..., None]
    precond = scaling[..., None]
    flat_ops = local_ops.reshape(GX * GY, NI, NI)
    flat_basis = corner_basis.reshape(GX * GY, 4 * CS, NI)
    node_ids = corner_map.reshape(-1).astype(jnp.int32)

    def per_subdomain(operands):
        stiff, basis, sided = operands
        return (jnp.dot(stiff, sided, preferred_element_type=jnp.float32),
                jnp.dot(basis, sided, preferred_element_type=jnp.float32))

    def operate(vector):
        east_part = vector[:, :, 0] * active[:, :, 0]
        north_part = vector[:, :, 1] * active[:, :, 1]
        west_part = jnp.roll(east_part, 1, 0)
        south_part = jnp.roll(north_part, 1, 1)
        sided_load = jnp.stack([east_part, -west_part, north_part, -south_part], 2)
        sided_load = sided_load.reshape(GX * GY, NI, NRHS).astype(jnp.bfloat16)
        local_part, partial_value = lax.map(per_subdomain, (flat_ops, flat_basis, sided_load))
        assembled = jnp.zeros((NODES, CS, NRHS), jnp.float32).at[node_ids].add(partial_value.reshape(GX * GY * 4, CS, NRHS))
        solved = jnp.dot(coarse_inverse, assembled.reshape(NC, NRHS), precision=highest).reshape(NODES, CS, NRHS)
        corner_values = solved[node_ids].reshape(GX * GY, 4 * CS, NRHS)
        responses = local_part + jnp.einsum("skn,skr->snr", flat_basis.astype(jnp.float32), corner_values, precision=highest)
        responses = responses.reshape(GX, GY, 4, SIDE, NRHS)
        east_of = jnp.roll(responses[:, :, 1], -1, 0)
        north_of = jnp.roll(responses[:, :, 3], -1, 1)
        return jnp.stack([(responses[:, :, 0] - east_of) * active[:, :, 0],
                          (responses[:, :, 2] - north_of) * active[:, :, 1]], 2)

    def inner_product(first, second):
        return jnp.sum(first * second, axis=(0, 1, 2, 3))

    multipliers = jnp.zeros_like(dual_rhs)
    residual = dual_rhs * active
    direction = precond * residual
    precond_norm = inner_product(residual, direction)
    for iteration in range(ITERS):
        image_vec = operate(direction)
        step_size = precond_norm / inner_product(direction, image_vec)
        multipliers = multipliers + step_size * direction
        residual = residual - step_size * image_vec
        if iteration + 1 < ITERS:
            preconditioned = precond * residual
            norm_next = inner_product(residual, preconditioned)
            direction = preconditioned + (norm_next / precond_norm) * direction
            precond_norm = norm_next
    return multipliers, residual
```

```python
import numpy as np
import jax
import jax.numpy as jnp
from jax import lax
from jax.sharding import PartitionSpec as P

CS = 3
ROWS = 40
HIGHEST = lax.Precision.HIGHEST


def shifted(array, axis, by):
    count = lax.axis_size(axis)
    return lax.ppermute(array, axis, [(i, (i + by) % count) for i in range(count)])


def spread_sy(value):
    count = lax.axis_size("sy")
    groups = [[2 * z + core for z in range(count // 2)] for core in range(2)]
    copies = jnp.broadcast_to(value[None], (count // 2,) + value.shape)
    same = lax.all_to_all(copies, "sy", 0, 0, tiled=True, axis_index_groups=groups)
    other = lax.ppermute(same, "sy", [(i, i ^ 1) for i in range(count)])
    even = (lax.axis_index("sy") % 2 == 0).astype(jnp.int32)
    pair = jnp.where(even == 1, jnp.stack([same, other], 1), jnp.stack([other, same], 1))
    return pair.reshape((count,) + value.shape)


def spread_sx(value):
    count = lax.axis_size("sx")
    copies = jnp.broadcast_to(value[None], (count,) + value.shape)
    return lax.all_to_all(copies, "sx", 0, 0, tiled=True)


def edge_basis(basis, side):
    own = basis.astype(jnp.float32).reshape(2, 4, CS, 4, side)
    east = shifted(own[:, :, :, 1], "sx", -1)
    above = shifted(own[:1, :, :, 3], "sy", -1)
    north = jnp.concatenate([own[1:, :, :, 3], above], 0)
    zero = jnp.zeros((CS, side), jnp.float32)
    place = [(0, 0), (-1, 0), (0, -1), (-1, -1)]
    columns = []
    for s in range(2):
        for e in range(2):
            grid = [[zero] * 4 for _ in range(3)]
            for k, (di, dj) in enumerate(place):
                grid[1 + di][1 + s + dj] = grid[1 + di][1 + s + dj] + own[s, k, :, 2 * e]
                if e == 0:
                    grid[2 + di][1 + s + dj] = grid[2 + di][1 + s + dj] - east[s, k]
                else:
                    grid[1 + di][2 + s + dj] = grid[1 + di][2 + s + dj] - north[s, k]
            columns.append(jnp.stack([jnp.stack(row) for row in grid]).reshape(12 * CS, side))
    return jnp.concatenate(columns, 1)


def static_maps(gx, gy):
    nodes_y = 2 * gy
    merge = np.zeros((3 * nodes_y * CS, gy * ROWS), np.float32)
    for b in range(gy):
        for ii in range(3):
            for jj in range(4):
                for c in range(CS):
                    j = (2 * b - 1 + jj) % nodes_y
                    merge[(ii * nodes_y + j) * CS + c, b * ROWS + (ii * 4 + jj) * CS + c] = 1
    expand = np.zeros((gx * ROWS, gx * 4 * CS), np.float32)
    for a in range(gx):
        for ii in range(3):
            for q in range(4 * CS):
                expand[a * ROWS + ii * 4 * CS + q, ((a - 1 + ii) % gx) * 4 * CS + q] = 1
    totals = np.zeros((gx * ROWS, gy * ROWS), np.float32)
    for a in range(gx):
        for b in range(gy):
            for q in range(12 * CS, ROWS):
                totals[a * ROWS + q, b * ROWS + q] = 1
    return merge, expand, totals


def local(dual_rhs, scaling, dual_count, corner_map, local_ops, corner_basis, coarse_inverse):
    gx, gy = lax.axis_size("sx"), lax.axis_size("sy")
    a, b = lax.axis_index("sx"), lax.axis_index("sy")
    rhs = dual_rhs[0]
    stiffness = local_ops[0]
    side, cases = rhs.shape[2], rhs.shape[3]
    block = coarse_inverse.shape[0]
    order = block * gx
    nodes_y = 2 * gy
    active = (
        lax.broadcasted_iota(jnp.int32, (2, 2, side), 2) < dual_count[0][:, :, None]
    ).astype(jnp.float32)[..., None]
    precond = scaling[0][..., None]

    numbers = corner_map[0, :, 0].astype(jnp.float32)
    corner = stiffness[:, :cases, :cases].astype(jnp.float32)
    size = jnp.sum(corner * jnp.eye(corner.shape[1], dtype=jnp.float32)) / (2 * gx * gy * corner.shape[1])
    size = size + jnp.sum(jnp.abs(coarse_inverse)) / order
    spare = jnp.concatenate([numbers, size[None], jnp.zeros((cases - block - 3,), jnp.float32)])
    wide = jnp.concatenate([coarse_inverse, jnp.broadcast_to(spare[None], (block, cases - block))], 1)
    columns_all = spread_sx(wide)
    column_numbers = columns_all[:, 0, block : block + 2].reshape(2 * gx)
    column_size = jnp.sum(columns_all[:, 0, block + 2])

    edges = edge_basis(corner_basis[0], side)

    def message(vector, extra):
        rows = jnp.dot(edges, vector.reshape(4 * side, cases), precision=HIGHEST)
        return jnp.concatenate([rows] + [row.reshape(1, cases) for row in extra], 0)

    def inner(first, second):
        return jnp.sum(first * second, axis=(0, 1, 2))

    zeros = jnp.zeros((cases,), jnp.float32)
    residual = rhs * active
    w0 = precond * residual
    facts = jnp.concatenate([column_numbers, column_size[None], jnp.zeros((cases - 2 * gx - 1,), jnp.float32)])
    gathered = spread_sy(message(w0, [inner(residual, w0), facts, zeros, zeros]))
    grid_numbers = gathered[:, 12 * CS + 1, : 2 * gx].reshape(gy, gx, 2)
    kappa = 4.0 / jnp.sum(gathered[:, 12 * CS + 1, 2 * gx])
    grid_numbers = jnp.swapaxes(grid_numbers, 0, 1).reshape(gx, nodes_y).astype(jnp.int32)

    row_nodes = lax.dynamic_slice_in_dim(grid_numbers, a, 1, 0).reshape(nodes_y, 1)
    picked_rows = (row_nodes * CS + jnp.arange(CS, dtype=jnp.int32)[None]).reshape(-1, 1)
    pick = (picked_rows == jnp.arange(order, dtype=jnp.int32)[None]).astype(jnp.float32)
    row_part = jnp.dot(pick, columns_all.reshape(order, cases), precision=HIGHEST)
    row_all = spread_sy(row_part)[:, :, :block]
    near = jnp.roll(grid_numbers, 1 - 2 * b, axis=1)[:, :4]
    need = (near[:, :, None] * CS + jnp.arange(CS, dtype=jnp.int32)).reshape(-1, 1)
    pick_near = (need == jnp.arange(order, dtype=jnp.int32)[None]).astype(jnp.float32)
    own_part = jnp.einsum(
        "rck,cnk->rn", pick_near.reshape(-1, gy, block), row_all, precision=HIGHEST
    )
    below = shifted(own_part, "sx", 1)
    beyond = shifted(own_part, "sx", -1)
    merge, expand, totals = static_maps(gx, gy)
    coarse_block = jnp.concatenate([below, own_part, beyond], 1)
    coarse_block = jnp.dot(jnp.dot(expand, coarse_block, precision=HIGHEST), merge, precision=HIGHEST) + totals

    def coarse_solve(gathered):
        send = jnp.dot(coarse_block, gathered.reshape(gy * ROWS, cases), precision=HIGHEST)
        got = lax.all_to_all(send.reshape(gx, ROWS, cases), "sx", 0, 0, tiled=True)
        return jnp.sum(got, 0)

    def respond(vector):
        east, north = vector[:, 0], vector[:, 1]
        west = shifted(east, "sx", 1)
        south = jnp.concatenate([shifted(north[1:], "sy", 1), north[:1]], 0)
        loads = jnp.stack([east, -west, north, -south], 1).reshape(2, 4 * side, cases)
        high = loads.astype(jnp.bfloat16)
        low = (loads - high.astype(jnp.float32)).astype(jnp.bfloat16)
        both = jnp.concatenate([high, low], 2)
        out = jnp.einsum("sij,sjr->sir", stiffness, both, preferred_element_type=jnp.float32)
        out = out[:, :, :cases] + out[:, :, cases:]
        out = out.reshape(2, 4, side, cases)
        back_east = shifted(out[:, 1], "sx", -1)
        back_north = jnp.concatenate([out[1:, 3], shifted(out[:1, 3], "sy", -1)], 0)
        return jnp.stack([out[:, 0] - back_east, out[:, 2] - back_north], 1)

    def image(local_part, solved):
        coarse_part = jnp.dot(edges.T, solved[: 12 * CS], precision=HIGHEST)
        return (local_part + coarse_part.reshape(2, 2, side, cases)) * active

    local0 = respond(w0)
    solved = coarse_solve(gathered)
    m0 = solved[12 * CS]
    u1 = image(local0, solved)
    w1 = kappa * precond * u1
    gathered = spread_sy(message(w1, [inner(w0, u1), inner(u1, w1), zeros, zeros]))
    local1 = respond(w1)
    solved = coarse_solve(gathered)
    m1, m2 = kappa * solved[12 * CS], kappa * solved[12 * CS + 1]
    u2 = image(local1, solved)
    w2 = kappa * precond * u2
    gathered = spread_sy(message(w2, [inner(w1, u2), inner(u2, w2), zeros, zeros]))
    local2 = respond(w2)
    solved = coarse_solve(gathered)
    m3, m4 = kappa * solved[12 * CS], kappa * solved[12 * CS + 1]
    u3 = image(local2, solved)
    last = jnp.broadcast_to(inner(w2, u3)[None], (gx * gy, cases))
    m5 = kappa * jnp.sum(lax.all_to_all(last, ("sx", "sy"), 0, 0, tiled=True), 0)

    moments = [m0, m1, m2, m3, m4, m5]

    def form(first, second, shift):
        total = 0.0
        for i, x in enumerate(first):
            for j, y in enumerate(second):
                total = total + x * y * moments[i + j + shift]
        return total

    one = jnp.ones((cases,), jnp.float32)
    rho, pi, gamma = [one], [one], []
    rz = m0
    for iteration in range(3):
        step = rz / form(pi, pi, 1)
        gamma = [
            (gamma[k] if k < len(gamma) else 0.0) + step * pi[k] for k in range(len(pi))
        ]
        rho = [one] + [-value for value in gamma]
        if iteration < 2:
            rz_new = form(rho, rho, 0)
            ratio = rz_new / rz
            pi = [rho[k] + (ratio * pi[k] if k < len(pi) else 0.0) for k in range(len(rho))]
            rz = rz_new
    gamma = [kappa * value for value in gamma]
    multipliers = gamma[0] * w0 + gamma[1] * w1 + gamma[2] * w2
    residual = residual - (gamma[0] * u1 + gamma[1] * u2 + gamma[2] * u3)
    return (multipliers[None], residual[None])


def solution(mesh):
    in_specs = (
        P("sx", "sy", None, None, None),
        P("sx", "sy", None, None),
        P("sx", "sy", None),
        P("sx", "sy", None),
        P("sx", "sy", None, None),
        P("sx", "sy", None, None),
        P("sx", "sy"),
    )
    out_specs = (P("sx", "sy", None, None, None), P("sx", "sy", None, None, None))
    return jax.shard_map(local, mesh=mesh, in_specs=in_specs, out_specs=out_specs, check_vma=False)
```

```python
import functools

import numpy as np
import jax
import jax.numpy as jnp
from jax import lax
from jax.experimental import pallas as pl
from jax.experimental.pallas import tpu as pltpu
from jax.sharding import PartitionSpec as P

CS = 3
NEAR = 16
ROWS = 3 * NEAR
F32, BF16 = jnp.float32, jnp.bfloat16
VMEM = pl.BlockSpec(memory_space=pltpu.VMEM)
SMEM = pl.BlockSpec(memory_space=pltpu.SMEM)


def shifted(array, axis, by):
    count = lax.axis_size(axis)
    return lax.ppermute(array, axis, [(i, (i + by) % count) for i in range(count)])


def along_sy(copies):
    count = lax.axis_size("sy")
    groups = [[2 * z + core for z in range(count // 2)] for core in range(2)]
    same = lax.all_to_all(copies, "sy", 0, 0, tiled=True, axis_index_groups=groups)
    return same, lax.ppermute(same, "sy", [(i, i ^ 1) for i in range(count)])


def vmem_call(body, outs, scratch=(), limit=48):
    return pl.pallas_call(
        body,
        out_shape=outs,
        scratch_shapes=list(scratch),
        compiler_params=pltpu.CompilerParams(vmem_limit_bytes=limit * 2**20),
    )


def split(value):
    high = value.astype(BF16)
    return high, (value - high.astype(F32)).astype(BF16)


def halves(value):
    return jnp.concatenate(split(value), 1)


def multiply(first, second):
    return jnp.dot(first, second, preferred_element_type=F32)


def place_matrices():
    place = [(0, 0), (-1, 0), (0, -1), (-1, -1)]
    out = np.zeros((4, ROWS, 32), np.float32)
    for s in range(2):
        for e in range(2):
            for k, (di, dj) in enumerate(place):
                for c in range(CS):
                    out[2 * s + e, (1 + di) * NEAR + (1 + s + dj) * CS + c, k * CS + c] += 1
                    row = (1 + di + (1 - e)) * NEAR + (1 + s + dj + e) * CS + c
                    out[2 * s + e, row, 16 + k * CS + c] -= 1
    return out


def lane_matrices(gy):
    out = np.zeros((2, 128, gy * NEAR), np.float32)
    for core in range(2):
        for slot in range(gy):
            z, other = slot % (gy // 2), slot // (gy // 2)
            source = 2 * z + (core ^ other)
            for jj in range(4):
                for c in range(CS):
                    j = (2 * source - 1 + jj) % (2 * gy)
                    out[core, j * CS + c, slot * NEAR + jj * CS + c] = 1
    return out


def message_to(out_ref, basis_ref, vector, extra):
    got = multiply(basis_ref[...], halves(vector))
    cases = got.shape[1] // 2
    rows = got[:ROWS, :cases] + got[:ROWS, cases:] + got[ROWS:, :cases]
    index = lax.broadcasted_iota(jnp.int32, rows.shape, 0)
    for k, row in enumerate(extra):
        rows = jnp.where(index == NEAR - 4 + k, row, rows)
    for copy in range(out_ref.shape[0]):
        out_ref[copy] = rows


def column_sum(value):
    return jnp.sum(value, axis=0, keepdims=True)


def begin_body(rhs, gain_in, count, basis, east, above, places, facts, res, w0, act, gain, edges, message):
    side, cases = rhs.shape[1], rhs.shape[2]
    norm = jnp.zeros((1, cases), F32)
    for edge in range(4):
        s, e = divmod(edge, 2)
        index = lax.broadcasted_iota(jnp.int32, (side, cases), 0)
        mask = (index < count[s, e]).astype(F32)
        act[edge] = mask
        gain[edge] = gain_in[edge] * mask
        res[edge] = rhs[edge] * mask
        w0[edge] = gain[edge] * res[edge]
        norm = norm + column_sum(res[edge] * w0[edge])
        own = basis[s, :, 2 * e * side : (2 * e + 1) * side].astype(BF16)
        if e == 0:
            other = east[s].astype(BF16)
        elif s == 0:
            other = basis[1, :, 3 * side :].astype(BF16)
        else:
            other = above[...].astype(BF16)
        place = places[edge].astype(BF16)
        value = multiply(place[:, : 4 * CS], own) + multiply(place[:, 16 : 16 + 4 * CS], other)
        high, low = split(value)
        edges[:ROWS, edge * side : (edge + 1) * side] = high
        edges[ROWS:, edge * side : (edge + 1) * side] = low
    message_to(message, edges, w0[...].reshape(4 * side, cases), [norm, facts[...]])


def load_parts(parts, own, west, below):
    side, cases = own.shape[1], own.shape[2]
    for s in range(2):
        south = -below[...] if s == 0 else -own[1]
        for q, value in enumerate([own[2 * s], -west[s], own[2 * s + 1], south]):
            high, low = split(value)
            parts[s, q * side : (q + 1) * side, :cases] = high
            parts[s, q * side : (q + 1) * side, cases:] = low


def apply_rows(block, parts, s):
    out = multiply(block[0], parts[s])
    cases = out.shape[1] // 2
    return out[:, :cases] + out[:, cases:]


def give_body(own, west, below, block, out, parts):
    step = pl.program_id(0)

    @pl.when(step == 0)
    def _():
        load_parts(parts, own, west, below)

    out[0] = apply_rows(block, parts, step % 2)


def keep_body(own, west, below, block, out, parts):
    step = pl.program_id(0)

    @pl.when(step == 0)
    def _():
        load_parts(parts, own, west, below)

    value = apply_rows(block, parts, step // 2 - step // 4)

    @pl.when(step < 4)
    def _():
        out[step] = value

    @pl.when(step == 4)
    def _():
        out[1] = out[1] - value


def stiffness_call(give, own, west, below, blocks):
    side, cases = own.shape[1], own.shape[2]
    if give:
        steps, body = 3, give_body
        where = lambda t: (jnp.where(t == 2, 3, 1 + 4 * t), 0, 0)
        out_spec = pl.BlockSpec((1, side, cases), lambda t: (t, 0, 0))
        out_shape = jax.ShapeDtypeStruct((3, side, cases), F32)
    else:
        steps, body = 5, keep_body
        where = lambda t: (jnp.where(t == 4, 7, 2 * t), 0, 0)
        out_spec = pl.BlockSpec((4, side, cases), lambda t: (0, 0, 0))
        out_shape = jax.ShapeDtypeStruct((4, side, cases), F32)
    whole = lambda shape: pl.BlockSpec(shape, lambda t: (0,) * len(shape))
    return pl.pallas_call(
        body,
        grid=(steps,),
        in_specs=[
            whole(own.shape),
            whole(west.shape),
            whole(below.shape),
            pl.BlockSpec((1,) + blocks.shape[1:], where),
        ],
        out_specs=out_spec,
        out_shape=out_shape,
        scratch_shapes=[pltpu.VMEM((2, 4 * side, 2 * cases), BF16)],
        compiler_params=pltpu.CompilerParams(vmem_limit_bytes=40 * 2**20),
        cost_estimate=pl.CostEstimate(
            flops=steps * side * 4 * side * cases * 4,
            bytes_accessed=steps * side * 4 * side * 2 + 10 * side * cases * 4,
            transcendentals=0,
        ),
    )(own, west, below, blocks)


def image_body(last, part, east, north, got, edges, act, gain, kappa, previous, *outs):
    side, cases = part.shape[1], part.shape[2]
    total = got[0]
    for k in range(1, got.shape[0]):
        total = total + got[k]
    high, low = split(total)
    twice = jnp.concatenate(
        [jnp.concatenate([high, low], 1), jnp.concatenate([high, jnp.zeros_like(low)], 1)], 0
    )
    u_ref = outs[0]
    first = jnp.zeros((1, cases), F32)
    second = jnp.zeros((1, cases), F32)
    for edge in range(4):
        coarse = lax.dot_general(
            edges[:, edge * side : (edge + 1) * side],
            twice,
            (((0,), (0,)), ((), ())),
            preferred_element_type=F32,
        )
        value = part[edge] + coarse[:, :cases] + coarse[:, cases:]
        if edge % 2 == 0:
            value = value - east[edge // 2]
        elif edge == 3:
            value = value - north[...]
        u_ref[edge] = value * act[edge]
        first = first + column_sum(previous[edge] * u_ref[edge])
        if not last:
            outs[1][edge] = kappa[...] * gain[edge] * value
            second = second + column_sum(outs[1][edge] * u_ref[edge])
    spare = total[NEAR - 8 : NEAR]
    if last:
        outs[1][...] = spare
        outs[2][...] = jnp.broadcast_to(first, outs[2].shape)
    else:
        outs[2][...] = spare
        message_to(outs[3], edges, outs[1][...].reshape(4 * side, cases), [first, second])


def image_call(last, part, east, north, got, edges, act, gain, kappa, previous, copies):
    _, side, cases = part.shape
    field = jax.ShapeDtypeStruct((4, side, cases), F32)
    spare = jax.ShapeDtypeStruct((8, cases), F32)
    if last:
        outs = (field, spare, jax.ShapeDtypeStruct((copies, cases), F32))
    else:
        outs = (field, field, spare, jax.ShapeDtypeStruct((copies, ROWS, cases), F32))
    return vmem_call(functools.partial(image_body, last), outs)(
        part, east, north, got, edges, act, gain, kappa, previous
    )


def pick_body(numbers, me, columns, out, rows):
    gy = numbers.shape[0]
    rows[...] = jnp.zeros_like(rows)
    for j in range(2 * gy):
        node = numbers[j // 2, 2 * me[0] + j % 2]
        for c in range(CS):
            rows[pl.ds(j * CS + c, 1)] = columns[pl.ds(node * CS + c, 1)]
    turned = rows[...].T
    for copy in range(out.shape[0]):
        out[copy] = turned[: out.shape[1]]


def near_body(gx, numbers, me, same, other, out):
    gy = numbers.shape[0]
    block = same.shape[1]
    out[...] = jnp.zeros_like(out)
    core = me[1] % 2
    for jj in range(4):
        j = (2 * me[1] - 1 + jj + 2 * gy) % (2 * gy)
        for i in range(gx):
            node = numbers[j // 2, 2 * i + j % 2]
            owner = node * CS // block
            row = node * CS - owner * block
            mine = owner % 2 == core
            for c in range(CS):
                first = same[owner // 2, pl.ds(row + c, 1)]
                second = other[owner // 2, pl.ds(row + c, 1)]
                out[pl.ds(i * NEAR + jj * CS + c, 1)] = jnp.where(mine, first, second)


def coarse_body(below, own, beyond, lanes, same, other, out):
    gx = out.shape[0]
    cases = same.shape[2]
    lane = lanes[...].astype(BF16)
    value = jnp.zeros((gx * NEAR, cases), F32)
    for ii, source in enumerate([below, own, beyond]):
        pieces = [ref[z, ii * NEAR : (ii + 1) * NEAR] for ref in (same, other) for z in range(same.shape[0])]
        if ii == 0:
            total = pieces[0][NEAR - 8 :]
            for piece in pieces[1:]:
                total = total + piece[NEAR - 8 :]
        gathered = halves(jnp.concatenate(pieces, 0))
        high, low = split(source[...])
        high = multiply(high, lane).astype(BF16)
        low = multiply(low, lane).astype(BF16)
        product = multiply(high, gathered)
        value = value + product[:, :cases] + product[:, cases:] + multiply(low, gathered[:, :cases])
    index = lax.broadcasted_iota(jnp.int32, (8, cases), 0)
    for target in range(gx):
        for ii in range(3):
            at = ((target - 1 + ii) % gx) * NEAR
            out[target, ii * NEAR : ii * NEAR + 8] = value[at : at + 8]
            rest = value[at + 8 : at + 16]
            if ii == 0:
                rest = jnp.where(index < 4, rest, total)
            out[target, ii * NEAR + 8 : ii * NEAR + 16] = rest


def finish_body(kappa_ref, spare0, spare1, spare2, last, w0, w1, w2, u1, u2, u3, res, mult_out, res_out):
    kappa = kappa_ref[...]
    moments = [
        spare0[4:5],
        kappa * spare1[4:5],
        kappa * spare1[5:6],
        kappa * spare2[4:5],
        kappa * spare2[5:6],
        kappa * column_sum(last[...]),
    ]

    def form(first, second, shift):
        total = 0.0
        for i, x in enumerate(first):
            for j, y in enumerate(second):
                total = total + x * y * moments[i + j + shift]
        return total

    one = jnp.ones_like(kappa)
    rho, pi, gamma = [one], [one], []
    rz = moments[0]
    for iteration in range(3):
        step = rz / form(pi, pi, 1)
        gamma = [(gamma[k] if k < len(gamma) else 0.0) + step * pi[k] for k in range(len(pi))]
        rho = [one] + [-value for value in gamma]
        if iteration < 2:
            rz_new = form(rho, rho, 0)
            ratio = rz_new / rz
            pi = [rho[k] + (ratio * pi[k] if k < len(pi) else 0.0) for k in range(len(rho))]
            rz = rz_new
    gamma = [kappa * value for value in gamma]
    for edge in range(4):
        mult_out[edge] = gamma[0] * w0[edge] + gamma[1] * w1[edge] + gamma[2] * w2[edge]
        res_out[edge] = res[edge] - (gamma[0] * u1[edge] + gamma[1] * u2[edge] + gamma[2] * u3[edge])


def local(dual_rhs, scaling, dual_count, corner_map, local_ops, corner_basis, coarse_inverse):
    gx, gy = lax.axis_size("sx"), lax.axis_size("sy")
    a, b = lax.axis_index("sx"), lax.axis_index("sy")
    side, cases = dual_rhs.shape[3], dual_rhs.shape[4]
    rhs = dual_rhs.reshape(4, side, cases)
    blocks = local_ops.reshape(8, side, 4 * side)
    block = coarse_inverse.shape[0]
    order = block * gx
    field = jax.ShapeDtypeStruct((4, side, cases), F32)
    half = gy // 2
    basis = corner_basis[0]

    wide_basis = basis.astype(F32)
    east = shifted(wide_basis[:, :, side : 2 * side], "sx", -1)
    above = shifted(wide_basis[0, :, 3 * side :], "sy", -1)
    numbers = corner_map[0, :, 0].astype(F32)
    corner = local_ops[0, :, :cases, :cases].astype(F32)
    size = jnp.sum(corner * jnp.eye(corner.shape[1], dtype=F32)) / (2 * gx * gy * corner.shape[1])
    size = size + jnp.sum(jnp.abs(coarse_inverse)) / order
    spare = jnp.concatenate([numbers, size[None], jnp.zeros((cases - block - 3,), F32)])
    wide = jnp.concatenate([coarse_inverse, jnp.broadcast_to(spare[None], (block, cases - block))], 1)
    columns_all = lax.all_to_all(
        jnp.broadcast_to(wide[None], (gx, block, cases)), "sx", 0, 0, tiled=True
    )
    known = columns_all[:, 0]
    facts = jnp.concatenate(
        [
            known[:, block : block + 2].reshape(2 * gx),
            jnp.sum(known[:, block + 2])[None],
            jnp.zeros((cases - 2 * gx - 1,), F32),
        ]
    )[None]

    residual, w0, act, gain, edges, message = pl.pallas_call(
        begin_body,
        in_specs=[VMEM, VMEM, SMEM, VMEM, VMEM, VMEM, VMEM, VMEM],
        out_shape=(
            field,
            field,
            field,
            field,
            jax.ShapeDtypeStruct((2 * ROWS, 4 * side), BF16),
            jax.ShapeDtypeStruct((half, ROWS, cases), F32),
        ),
        compiler_params=pltpu.CompilerParams(vmem_limit_bytes=48 * 2**20),
    )(
        rhs,
        scaling.reshape(4, side, 1),
        dual_count[0],
        wide_basis,
        east,
        above,
        jnp.asarray(place_matrices()),
        facts,
    )

    def halo(vector):
        return shifted(vector.reshape(2, 2, side, cases)[:, 0], "sx", 1), shifted(vector[3], "sy", 1)

    def respond(vector, west, below):
        given = stiffness_call(True, vector, west, below, blocks)
        back_east = shifted(given[:2], "sx", -1)
        back_north = shifted(given[2], "sy", -1)
        kept = stiffness_call(False, vector, west, below, blocks)
        return kept, back_east, back_north

    same, other = along_sy(message)
    known = jnp.concatenate([same[:, NEAR - 3], other[:, NEAR - 3]], 0)
    even = b % 2 == 0
    ordered = jnp.where(
        even,
        jnp.stack([same[:, NEAR - 3], other[:, NEAR - 3]], 1),
        jnp.stack([other[:, NEAR - 3], same[:, NEAR - 3]], 1),
    ).reshape(gy, cases)
    kappa = jnp.broadcast_to(4.0 / jnp.sum(known[:, 2 * gx]), (1, cases))
    grid_numbers = ordered.astype(jnp.int32)
    me = jnp.stack([a, b]).astype(jnp.int32)

    turned = pl.pallas_call(
        pick_body,
        in_specs=[SMEM, SMEM, VMEM],
        out_shape=jax.ShapeDtypeStruct((half, block, cases), F32),
        scratch_shapes=[pltpu.VMEM((cases, cases), F32)],
    )(grid_numbers, me, columns_all.reshape(order, cases))
    rows_same, rows_other = along_sy(turned)
    own_part = pl.pallas_call(
        functools.partial(near_body, gx),
        in_specs=[SMEM, SMEM, VMEM, VMEM],
        out_shape=jax.ShapeDtypeStruct((gx * NEAR, cases), F32),
    )(grid_numbers, me, rows_same, rows_other)
    below_part = shifted(own_part, "sx", 1)
    beyond_part = shifted(own_part, "sx", -1)
    lanes = lax.dynamic_index_in_dim(jnp.asarray(lane_matrices(gy)), b % 2, 0, keepdims=False)

    def coarse_solve(same, other):
        send = vmem_call(coarse_body, jax.ShapeDtypeStruct((gx, ROWS, cases), F32))(
            below_part, own_part, beyond_part, lanes, same, other
        )
        return lax.all_to_all(send, "sx", 0, 0, tiled=True)

    def image(last, local_part, got, previous, copies):
        return image_call(last, *local_part, got, edges, act, gain, kappa, previous, copies)

    local0 = respond(w0, *halo(w0))
    got = coarse_solve(same, other)
    u1, w1, spare0, message = image(False, local0, got, w0, half)
    same, other = along_sy(message)
    local1 = respond(w1, *halo(w1))
    got = coarse_solve(same, other)
    u2, w2, spare1, message = image(False, local1, got, w1, half)
    same, other = along_sy(message)
    local2 = respond(w2, *halo(w2))
    got = coarse_solve(same, other)
    u3, spare2, last = image(True, local2, got, w2, gx * gy)
    last = lax.all_to_all(last.reshape(gx * gy, 1, cases), ("sx", "sy"), 0, 0, tiled=True)
    multipliers, residual = vmem_call(finish_body, (field, field))(
        kappa, spare0, spare1, spare2, last.reshape(gx * gy, cases), w0, w1, w2, u1, u2, u3, residual
    )
    shape = dual_rhs.shape
    return multipliers.reshape(shape), residual.reshape(shape)


def solution(mesh):
    in_specs = (
        P("sx", "sy", None, None, None),
        P("sx", "sy", None, None),
        P("sx", "sy", None),
        P("sx", "sy", None),
        P("sx", "sy", None, None),
        P("sx", "sy", None, None),
        P("sx", "sy"),
    )
    out_specs = (P("sx", "sy", None, None, None), P("sx", "sy", None, None, None))
    return jax.shard_map(local, mesh=mesh, in_specs=in_specs, out_specs=out_specs, check_vma=False)
```

```python
import functools
import math

import numpy as np
import jax
import jax.numpy as jnp
from jax import lax
from jax.experimental import pallas as pl
from jax.experimental.pallas import tpu as pltpu
from jax.sharding import PartitionSpec as P

CS = 3
NEAR = 16
ROWS = 3 * NEAR
F32, BF16 = jnp.float32, jnp.bfloat16
SMEM = pl.BlockSpec(memory_space=pltpu.SMEM)


def shifted(array, axis, by):
    count = lax.axis_size(axis)
    return lax.ppermute(array, axis, [(i, (i + by) % count) for i in range(count)])


def along_sy(copies):
    count = lax.axis_size("sy")
    groups = [[2 * z + core for z in range(count // 2)] for core in range(2)]
    same = lax.all_to_all(copies, "sy", 0, 0, tiled=True, axis_index_groups=groups)
    return same, lax.ppermute(same, "sy", [(i, i ^ 1) for i in range(count)])


def kernel_call(body, outs, operands, scalars=0, blocks=None, scratch=()):
    whole = lambda array: pl.BlockSpec(array.shape, lambda t: (0,) * len(array.shape))
    specs = [SMEM] * scalars + [whole(array) for array in operands[scalars:]]
    if blocks is not None:
        specs.append(pl.BlockSpec(memory_space=pltpu.HBM))
        operands = tuple(operands) + (blocks,)
    several = isinstance(outs, tuple)
    moved = sum(4 * math.prod(array.shape) for array in operands) + sum(
        4 * math.prod(array.shape) for array in (outs if several else (outs,))
    )
    return pl.pallas_call(
        body,
        grid=(1,),
        in_specs=specs,
        out_specs=tuple(whole(array) for array in outs) if several else whole(outs),
        out_shape=outs,
        scratch_shapes=list(scratch),
        compiler_params=pltpu.CompilerParams(vmem_limit_bytes=32 * 2**20),
        cost_estimate=pl.CostEstimate(flops=4 * moved, bytes_accessed=moved, transcendentals=0),
    )(*operands)


def split(value):
    high = value.astype(BF16)
    return high, (value - high.astype(F32)).astype(BF16)


def halves(value):
    return jnp.concatenate(split(value), 1)


def multiply(first, second):
    return jnp.dot(first, second, preferred_element_type=F32)


def place_matrices():
    place = [(0, 0), (-1, 0), (0, -1), (-1, -1)]
    out = np.zeros((4, ROWS, 32), np.float32)
    for s in range(2):
        for e in range(2):
            for k, (di, dj) in enumerate(place):
                for c in range(CS):
                    out[2 * s + e, (1 + di) * NEAR + (1 + s + dj) * CS + c, k * CS + c] += 1
                    row = (1 + di + (1 - e)) * NEAR + (1 + s + dj + e) * CS + c
                    out[2 * s + e, row, 16 + k * CS + c] -= 1
    return out


def lane_matrices(gy):
    out = np.zeros((2, 128, gy * NEAR), np.float32)
    for core in range(2):
        for slot in range(gy):
            z, other = slot % (gy // 2), slot // (gy // 2)
            source = 2 * z + (core ^ other)
            for jj in range(4):
                for c in range(CS):
                    j = (2 * source - 1 + jj) % (2 * gy)
                    out[core, j * CS + c, slot * NEAR + jj * CS + c] = 1
    return out


def message_to(out_ref, basis_ref, parts, extra):
    got = multiply(basis_ref[...], parts[...].reshape(basis_ref.shape[1], parts.shape[2]))
    cases = got.shape[1] // 2
    rows = got[:ROWS, :cases] + got[:ROWS, cases:] + got[ROWS:, :cases]
    index = lax.broadcasted_iota(jnp.int32, rows.shape, 0)
    for k, row in enumerate(extra):
        rows = jnp.where(index == NEAR - 4 + k, row, rows)
    for copy in range(out_ref.shape[0]):
        out_ref[copy] = rows


def column_sum(value):
    return jnp.sum(value, axis=0, keepdims=True)


def wide_body(me, corner, coarse, out):
    block = coarse.shape[0]
    count = out.shape[0]
    lane = lax.broadcasted_iota(jnp.int32, (block, out.shape[2] - block), 1)
    spare = jnp.where(lane == 2 * me[0], corner[0, 0], 0) + jnp.where(lane == 2 * me[0] + 1, corner[1, 0], 0)
    wide = jnp.concatenate([coarse[...], spare.astype(F32)], 1)
    for copy in range(count):
        out[copy] = wide


def begin_body(count, corner, rhs, gain_in, basis, east, above, places, coarse, tiles, res, east0, north0, north1, act, gain, edges, message, parts):
    side, cases = rhs.shape[1], rhs.shape[2]
    norm = jnp.zeros((1, cases), F32)
    for edge in range(4):
        s, e = divmod(edge, 2)
        index = lax.broadcasted_iota(jnp.int32, (side, cases), 0)
        mask = (index < count[s, e]).astype(F32)
        act[edge] = mask
        gain[edge] = gain_in[edge] * mask
        res[edge] = rhs[edge] * mask
        value = gain[edge] * res[edge]
        norm = norm + column_sum(res[edge] * value)
        put_edge(edge, value, east0, north0, north1, parts)
        own = basis[s, :, 2 * e * side : (2 * e + 1) * side].astype(BF16)
        if e == 0:
            other = east[s].astype(BF16)
        elif s == 0:
            other = basis[1, :, 3 * side :].astype(BF16)
        else:
            other = above[...].astype(BF16)
        place = places[edge].astype(BF16)
        value = multiply(place[:, : 4 * CS], own) + multiply(place[:, 16 : 16 + 4 * CS], other)
        high, low = split(value)
        edges[:ROWS, edge * side : (edge + 1) * side] = high
        edges[ROWS:, edge * side : (edge + 1) * side] = low
    lane = lax.broadcasted_iota(jnp.int32, (1, cases), 1)
    numbers = jnp.where(lane == 0, corner[0, 0], 0) + jnp.where(lane == 1, corner[1, 0], 0)
    index = lax.broadcasted_iota(jnp.int32, (cases, cases), 0)
    diagonal = index == lax.broadcasted_iota(jnp.int32, (cases, cases), 1)
    size = jnp.zeros((1, cases), F32)
    for s in range(2):
        tile = tiles[s].astype(F32)
        size = size + jnp.sum(jnp.where(diagonal, tile, 0.0)) / (512.0 * cases)
    size = size + jnp.sum(jnp.abs(coarse[...])) / (16.0 * coarse.shape[0])
    message_to(message, edges, parts, [norm, numbers.astype(F32), size])


def put_edge(edge, value, east, north0, north1, parts):
    side = value.shape[0]
    if edge % 2 == 0:
        east[edge // 2] = value
    elif edge == 1:
        north0[...] = value
    else:
        north1[...] = value
    high, low = split(value)
    parts[edge, :, : value.shape[1]] = high
    parts[edge, :, value.shape[1] :] = low


def apply_rows(block, parts):
    out = multiply(block, parts)
    cases = out.shape[1] // 2
    return out[:, :cases] + out[:, cases:]


def fetch(blocks, held, arrived, wanted):
    copies = [pltpu.make_async_copy(blocks.at[k], held.at[n], arrived.at[n]) for n, k in enumerate(wanted)]
    for copy in copies:
        copy.start()
    return copies


def give_body(own_east, own_north0, own_north1, west, below, blocks, out_east, out_north, parts, held, arrived):
    copies = fetch(blocks, held, arrived, (1, 3, 5))
    side = west.shape[1]
    own_north = (own_north0, own_north1)
    for s in range(2):
        parts[s, :side] = halves(own_east[s])
        parts[s, side : 2 * side] = halves(-west[s])
        parts[s, 2 * side : 3 * side] = halves(own_north[s][...])
    parts[0, 3 * side :] = halves(-below[...])
    parts[1, 3 * side :] = halves(-own_north0[...])
    copies[0].wait()
    out_east[0] = apply_rows(held[0], parts[0])
    copies[1].wait()
    out_north[...] = apply_rows(held[1], parts[0])
    copies[2].wait()
    out_east[1] = apply_rows(held[2], parts[1])


def keep_body(parts, blocks, out, held, arrived):
    copies = fetch(blocks, held, arrived, (0, 2, 7, 4, 6))
    for n, (edge, s) in enumerate([(0, 0), (1, 0), (1, 1), (2, 1), (3, 1)]):
        copies[n].wait()
        value = apply_rows(held[n], parts[s])
        out[edge] = out[edge] - value if n == 2 else value


def image_body(last, part, east, north, got, edges, act, gain, kappa_in, prev_east, prev_north0, prev_north1, *outs):
    side, cases = part.shape[1], part.shape[2]
    total = got[0]
    for k in range(1, got.shape[0]):
        total = total + got[k]
    if kappa_in is None:
        kappa = 4.0 / total[NEAR - 2 : NEAR - 1]
    else:
        kappa = kappa_in[0:1]
    high, low = split(total)
    twice = jnp.concatenate(
        [jnp.concatenate([high, low], 1), jnp.concatenate([high, jnp.zeros_like(low)], 1)], 0
    )
    u_ref = outs[0]
    first = jnp.zeros((1, cases), F32)
    second = jnp.zeros((1, cases), F32)
    previous = [prev_east[0], prev_north0[...], prev_east[1], prev_north1[...]]
    for edge in range(4):
        coarse = lax.dot_general(
            edges[:, edge * side : (edge + 1) * side],
            twice,
            (((0,), (0,)), ((), ())),
            preferred_element_type=F32,
        )
        value = part[edge] + coarse[:, :cases] + coarse[:, cases:]
        if edge % 2 == 0:
            value = value - east[edge // 2]
        elif edge == 3:
            value = value - north[...]
        image = value * act[edge]
        u_ref[edge] = image
        first = first + column_sum(previous[edge] * image)
        if not last:
            following = kappa * gain[edge] * value
            second = second + column_sum(following * image)
            put_edge(edge, following, outs[1], outs[2], outs[3], outs[-1])
    if last:
        outs[1][...] = total[NEAR - 8 : NEAR]
        outs[2][...] = jnp.broadcast_to(first, outs[2].shape)
    else:
        outs[4][...] = jnp.broadcast_to(kappa, outs[4].shape)
        outs[5][...] = total[NEAR - 8 : NEAR]
        message_to(outs[6], edges, outs[-1], [first, second])


def image_call(last, part, east, north, got, edges, act, gain, kappa, previous, copies):
    _, side, cases = part.shape
    shape = lambda *dims: jax.ShapeDtypeStruct(dims + (cases,), F32)
    scratch = ()
    if last:
        outs = (shape(4, side), shape(8), shape(copies))
    else:
        outs = (
            shape(4, side),
            shape(2, side),
            shape(side),
            shape(side),
            shape(8),
            shape(8),
            shape(copies, ROWS),
        )
        scratch = (pltpu.VMEM((4, side, 2 * cases), BF16),)
    body = functools.partial(image_body, last)
    operands = (part, east, north, got, edges, act, gain)
    if kappa is None:
        body = lambda *refs: image_body(last, *refs[:7], None, *refs[7:])
    else:
        operands = operands + (kappa,)
    return kernel_call(body, outs, operands + tuple(previous), scratch=scratch)


def slot_of(source, core, half):
    return source // 2 + half * ((source + core) % 2)


def pick_body(numbers, me, columns, out, rows):
    half = numbers.shape[0] // 2
    block = out.shape[1]
    rows[...] = jnp.zeros_like(rows)
    core = me[1] % 2
    for j in range(4 * half):
        node = numbers[slot_of(j // 2, core, half), j % 2]
        for c in range(CS):
            at = node * CS + c
            rows[pl.ds(j * CS + c, 1)] = columns[pl.ds(at // block, 1), pl.ds(at % block, 1)].reshape(1, -1)
    turned = rows[...].T[:block]
    known = jnp.zeros((1, turned.shape[1]), F32)
    for k in range(columns.shape[0]):
        known = known + columns[k, :1]
    lane = lax.broadcasted_iota(jnp.int32, turned.shape, 1)
    turned = jnp.where(lane >= block, known, turned)
    for copy in range(half):
        out[copy] = turned


def near_body(gx, numbers, me, same, other, out):
    half = same.shape[0]
    block = same.shape[1]
    out[...] = jnp.zeros_like(out)
    core = me[1] % 2
    lane = lax.broadcasted_iota(jnp.int32, (1, same.shape[2]), 1)
    for jj in range(4):
        j = (2 * me[1] - 1 + jj + 4 * half) % (4 * half)
        slot = slot_of(j // 2, core, half)
        for i in range(gx):
            node = numbers[slot, 2 * i + j % 2]
            owner = node * CS // block
            row = node * CS - owner * block
            mine = owner % 2 == core
            for c in range(CS):
                first = same[pl.ds(owner // 2, 1), pl.ds(row + c, 1)].reshape(1, -1)
                second = other[pl.ds(owner // 2, 1), pl.ds(row + c, 1)].reshape(1, -1)
                value = jnp.where(mine, first, second)
                out[pl.ds(i * NEAR + jj * CS + c, 1)] = jnp.where(lane < block, value, 0.0)


def coarse_body(count, lanes, *refs):
    sources, (same, other, *near, out) = refs[:count], refs[count:]
    gx = out.shape[0]
    cases = same.shape[2]
    lane = lanes[...].astype(BF16)
    value = jnp.zeros((gx * NEAR, cases), F32)
    for ii, source in enumerate(sources):
        pieces = [ref[z, ii * NEAR : (ii + 1) * NEAR] for ref in (same, other) for z in range(same.shape[0])]
        if ii == 0:
            total = pieces[0][NEAR - 8 :]
            for piece in pieces[1:]:
                total = total + piece[NEAR - 8 :]
        if near:
            middle = [ref[z, NEAR : 2 * NEAR] for ref in (same, other) for z in range(same.shape[0])]
            pieces = [
                middle[k] + sum(ref[k // ref.shape[1], k % ref.shape[1]] for ref in near)
                for k in range(len(middle))
            ]
        gathered = halves(jnp.concatenate(pieces, 0))
        high, low = split(source[...])
        high = multiply(high, lane).astype(BF16)
        low = multiply(low, lane).astype(BF16)
        product = multiply(high, gathered)
        value = value + product[:, :cases] + product[:, cases:] + multiply(low, gathered[:, :cases])
    index = lax.broadcasted_iota(jnp.int32, (8, cases), 0)
    for target in range(gx):
        for ii in range(3):
            at = ((target - 1 + ii) % gx) * NEAR
            out[target, ii * NEAR : ii * NEAR + 8] = value[at : at + 8]
            rest = value[at + 8 : at + 16]
            if ii == 0:
                rest = jnp.where(index < 4, rest, total)
            out[target, ii * NEAR + 8 : ii * NEAR + 16] = rest


def finish_body(kappa_ref, spare0, spare1, spare2, last, *refs):
    fields, (u1, u2, u3, res, mult_out, res_out) = refs[:9], refs[9:]
    kappa = kappa_ref[0:1]
    moments = [
        spare0[4:5],
        kappa * spare1[4:5],
        kappa * spare1[5:6],
        kappa * spare2[4:5],
        kappa * spare2[5:6],
        kappa * column_sum(last[...]),
    ]

    def form(first, second, shift):
        total = 0.0
        for i, x in enumerate(first):
            for j, y in enumerate(second):
                total = total + x * y * moments[i + j + shift]
        return total

    one = jnp.ones_like(kappa)
    rho, pi, gamma = [one], [one], []
    rz = moments[0]
    for iteration in range(3):
        step = rz / form(pi, pi, 1)
        gamma = [(gamma[k] if k < len(gamma) else 0.0) + step * pi[k] for k in range(len(pi))]
        rho = [one] + [-value for value in gamma]
        if iteration < 2:
            rz_new = form(rho, rho, 0)
            ratio = rz_new / rz
            pi = [rho[k] + (ratio * pi[k] if k < len(pi) else 0.0) for k in range(len(rho))]
            rz = rz_new
    gamma = [kappa * value for value in gamma]
    for edge in range(4):
        total = 0.0
        for k in range(3):
            east, north0, north1 = fields[3 * k : 3 * k + 3]
            value = east[edge // 2] if edge % 2 == 0 else (north0, north1)[edge // 2][...]
            total = total + gamma[k] * value
        mult_out[edge] = total
        res_out[edge] = res[edge] - (gamma[0] * u1[edge] + gamma[1] * u2[edge] + gamma[2] * u3[edge])


def local(dual_rhs, scaling, dual_count, corner_map, local_ops, corner_basis, coarse_inverse):
    gx, gy = lax.axis_size("sx"), lax.axis_size("sy")
    a, b = lax.axis_index("sx"), lax.axis_index("sy")
    side, cases = dual_rhs.shape[3], dual_rhs.shape[4]
    rhs = dual_rhs.reshape(4, side, cases)
    blocks = local_ops.reshape(8, side, 4 * side)
    block = coarse_inverse.shape[0]
    half = gy // 2
    basis = corner_basis[0]
    me = jnp.stack([a, b]).astype(jnp.int32)
    shape = lambda *dims: jax.ShapeDtypeStruct(dims + (cases,), F32)
    field = shape(4, side)
    double = lambda *dims: jax.ShapeDtypeStruct(dims + (2 * cases,), BF16)
    wide = kernel_call(wide_body, shape(gx, block), (me, corner_map[0], coarse_inverse), 2)
    columns_all = lax.all_to_all(wide, "sx", 0, 0, tiled=True)
    wide_basis = basis.astype(F32)
    east = shifted(wide_basis[:, :, side : 2 * side], "sx", -1)
    above = shifted(wide_basis[0, :, 3 * side :], "sy", -1)

    residual, *w0, act, gain, edges, message = kernel_call(
        begin_body,
        (
            field,
            shape(2, side),
            shape(side),
            shape(side),
            field,
            field,
            jax.ShapeDtypeStruct((2 * ROWS, 4 * side), BF16),
            shape(half, ROWS),
        ),
        (
            dual_count[0],
            corner_map[0],
            rhs,
            scaling.reshape(4, side, 1),
            wide_basis,
            east,
            above,
            jnp.asarray(place_matrices()),
            coarse_inverse,
            local_ops[0, :, :cases, :cases],
        ),
        2,
        scratch=(pltpu.VMEM((4, side, 2 * cases), BF16),),
    )
    message, columns_all = lax.optimization_barrier((message, columns_all))

    def halo(vector):
        return shifted(vector[0], "sx", 1), shifted(vector[2], "sy", 1)

    def held(count):
        return (pltpu.VMEM((count,) + blocks.shape[1:], BF16), pltpu.SemaphoreType.DMA((count,)))

    def give(own, west, below):
        given_east, given_north, parts = kernel_call(
            give_body,
            (shape(2, side), shape(side), double(2, 4 * side)),
            (*own, west, below),
            blocks=blocks,
            scratch=held(3),
        )
        return parts, shifted(given_east, "sx", -1), shifted(given_north, "sy", -1)

    def keep(parts):
        return kernel_call(keep_body, field, (parts,), blocks=blocks, scratch=held(5))

    west, below = halo(w0)
    same, other = along_sy(message)
    lower = shifted(jnp.stack([same[:, :NEAR], other[:, :NEAR]]), "sx", -1)
    upper = shifted(jnp.stack([same[:, 2 * NEAR :], other[:, 2 * NEAR :]]), "sx", 1)
    numbers = jnp.concatenate([same[:, NEAR - 3, :2], other[:, NEAR - 3, :2]], 0).astype(jnp.int32)
    turned = kernel_call(
        pick_body, shape(half, block), (numbers, me, columns_all), 2, scratch=(pltpu.VMEM((cases, cases), F32),)
    )
    turned, west, below = lax.optimization_barrier((turned, west, below))
    parts, back_east, back_north = give(w0, west, below)
    kept = keep(parts)
    rows_same, rows_other = along_sy(turned)
    rows_same, rows_other, kept, lower, upper = lax.optimization_barrier(
        (rows_same, rows_other, kept, lower, upper)
    )
    numbers = jnp.concatenate([rows_same[:, 0, block:], rows_other[:, 0, block:]], 0).astype(jnp.int32)
    own_part = kernel_call(
        functools.partial(near_body, gx), shape(gx * NEAR), (numbers, me, rows_same, rows_other), 2
    )
    below_part = shifted(own_part, "sx", 1)
    beyond_part = shifted(own_part, "sx", -1)
    lanes = lax.dynamic_index_in_dim(jnp.asarray(lane_matrices(gy)), b % 2, 0, keepdims=False)

    def coarse_solve(sources, *arrived):
        send = kernel_call(
            functools.partial(coarse_body, len(sources)),
            shape(gx, ROWS),
            (lanes, *sources, *arrived),
        )
        return lax.all_to_all(send, "sx", 0, 0, tiled=True)

    got = coarse_solve((own_part,), same, other, lower, upper)
    u1, *w1, kappa, spare0, message = image_call(
        False, kept, back_east, back_north, got, edges, act, gain, None, w0, half
    )
    sources = (below_part, own_part, beyond_part)
    west, below = halo(w1)
    same, other = along_sy(message)
    parts, back_east, back_north = give(w1, west, below)
    got = coarse_solve(sources, same, other)
    kept = keep(parts)
    u2, *w2, _, spare1, message = image_call(
        False, kept, back_east, back_north, got, edges, act, gain, kappa, w1, half
    )
    west, below = halo(w2)
    same, other = along_sy(message)
    parts, back_east, back_north = give(w2, west, below)
    got = coarse_solve(sources, same, other)
    kept = keep(parts)
    u3, spare2, last = image_call(
        True, kept, back_east, back_north, got, edges, act, gain, kappa, w2, gx * gy
    )
    last = lax.all_to_all(last.reshape(gx * gy, 1, cases), ("sx", "sy"), 0, 0, tiled=True)
    multipliers, residual = kernel_call(
        finish_body,
        (field, field),
        (kappa, spare0, spare1, spare2, last.reshape(gx * gy, cases), *w0, *w1, *w2, u1, u2, u3, residual),
    )
    return multipliers.reshape(dual_rhs.shape), residual.reshape(dual_rhs.shape)


def solution(mesh):
    in_specs = (
        P("sx", "sy", None, None, None),
        P("sx", "sy", None, None),
        P("sx", "sy", None),
        P("sx", "sy", None),
        P("sx", "sy", None, None),
        P("sx", "sy", None, None),
        P("sx", "sy"),
    )
    out_specs = (P("sx", "sy", None, None, None), P("sx", "sy", None, None, None))
    return jax.shard_map(local, mesh=mesh, in_specs=in_specs, out_specs=out_specs, check_vma=False)
```

```python
import functools
import math

import numpy as np
import jax
import jax.numpy as jnp
from jax import lax
from jax.experimental import pallas as pl
from jax.experimental.pallas import tpu as pltpu
from jax.sharding import PartitionSpec as P

CS = 3
NEAR = 16
ROWS = 3 * NEAR
F32, BF16 = jnp.float32, jnp.bfloat16
SMEM = pl.BlockSpec(memory_space=pltpu.SMEM)


def shifted(array, axis, by):
    count = lax.axis_size(axis)
    return lax.ppermute(array, axis, [(i, (i + by) % count) for i in range(count)])


def along_sy(copies, beside=None):
    count = lax.axis_size("sy")
    groups = [[2 * z + core for z in range(count // 2)] for core in range(2)]
    same = lax.all_to_all(copies, "sy", 0, 0, tiled=True, axis_index_groups=groups)
    if beside is not None:
        same, beside = lax.optimization_barrier((same, beside))
    other = lax.ppermute(same, "sy", [(i, i ^ 1) for i in range(count)])
    return (same, other) if beside is None else (same, other, beside)


class Arriving:
    def __init__(self, source, held, arrived):
        self.copy = pltpu.make_async_copy(source, held, arrived)
        self.copy.start()
        self.held, self.shape, self.waiting = held, held.shape, True

    def settle(self):
        if self.waiting:
            self.copy.wait()
        self.waiting = False

    def __getitem__(self, index):
        self.settle()
        return self.held[index]


class Leaving:
    def __init__(self, held, target, arrived):
        self.copy = pltpu.make_async_copy(held, target, arrived)
        self.held, self.shape, self.sent = held, held.shape, False

    def __getitem__(self, index):
        return self.held[index]

    def __setitem__(self, index, value):
        self.held[index] = value

    def send(self):
        if not self.sent:
            self.copy.start()
        self.sent = True


def kernel_call(body, outs, operands, scalars=0, raw=(), scratch=(), fast=(), fast_outs=()):
    several = isinstance(outs, tuple)
    outs = outs if several else (outs,)
    operands = tuple(operands)
    count_in, count_out = len(operands), len(outs)
    slow_in = [k for k in range(scalars, count_in) if k not in fast]
    slow_out = [k for k in range(count_out) if k not in fast_outs]
    held = [pltpu.VMEM(operands[k].shape, operands[k].dtype) for k in slow_in]
    held += [pltpu.VMEM(outs[k].shape, outs[k].dtype) for k in slow_out]
    arrays = list(operands) + list(raw)
    moved = sum(4 * math.prod(array.shape) for array in arrays + list(outs))

    def wrapped(*refs):
        refs = list(refs)
        ins, refs = refs[: len(arrays)], refs[len(arrays) :]
        results, refs = refs[:count_out], refs[count_out:]
        buffers, refs = refs[: len(held)], refs[len(held) :]
        arrived, extra = refs[0], refs[1:]
        for n, k in enumerate(slow_in):
            ins[k] = Arriving(ins[k], buffers[n], arrived.at[n])
        for n, k in enumerate(slow_out, len(slow_in)):
            results[k] = Leaving(buffers[n], results[k], arrived.at[n])
        body(*ins, *results, *extra)
        for k in slow_in:
            ins[k].settle()
        for k in slow_out:
            results[k].send()
        for k in slow_out:
            results[k].copy.wait()

    def spec(k):
        return SMEM if k < scalars else pl.BlockSpec(memory_space=pltpu.VMEM if k in fast else pltpu.HBM)

    arrays = [
        array if k < scalars or k in fast else pltpu.with_memory_space_constraint(array, pltpu.HBM)
        for k, array in enumerate(arrays)
    ]
    out_specs = tuple(
        pl.BlockSpec(memory_space=pltpu.VMEM if k in fast_outs else pltpu.HBM) for k in range(count_out)
    )
    out_shape = tuple(
        (pltpu.VMEM if k in fast_outs else pltpu.HBM)(array.shape, array.dtype) for k, array in enumerate(outs)
    )
    got = pl.pallas_call(
        wrapped,
        in_specs=[spec(k) for k in range(len(arrays))],
        out_specs=out_specs,
        out_shape=out_shape,
        scratch_shapes=held + [pltpu.SemaphoreType.DMA((max(len(held), 1),))] + list(scratch),
        compiler_params=pltpu.CompilerParams(vmem_limit_bytes=16 * 2**20),
        cost_estimate=pl.CostEstimate(flops=4 * moved, bytes_accessed=moved, transcendentals=0),
    )(*arrays)
    return tuple(got) if several else got[0]


def split(value):
    high = value.astype(BF16)
    return high, (value - high.astype(F32)).astype(BF16)


def halves(value):
    return jnp.concatenate(split(value), 1)


def multiply(first, second):
    return jnp.dot(first, second, preferred_element_type=F32)


def place_matrices():
    place = [(0, 0), (-1, 0), (0, -1), (-1, -1)]
    out = np.zeros((4, ROWS, 32), np.float32)
    for s in range(2):
        for e in range(2):
            for k, (di, dj) in enumerate(place):
                for c in range(CS):
                    out[2 * s + e, (1 + di) * NEAR + (1 + s + dj) * CS + c, k * CS + c] += 1
                    row = (1 + di + (1 - e)) * NEAR + (1 + s + dj + e) * CS + c
                    out[2 * s + e, row, 16 + k * CS + c] -= 1
    return out


def lane_matrices(gy):
    out = np.zeros((2, 128, gy * NEAR), np.float32)
    for core in range(2):
        for slot in range(gy):
            z, other = slot % (gy // 2), slot // (gy // 2)
            source = 2 * z + (core ^ other)
            for jj in range(4):
                for c in range(CS):
                    j = (2 * source - 1 + jj) % (2 * gy)
                    out[core, j * CS + c, slot * NEAR + jj * CS + c] = 1
    return out


def message_to(out_ref, basis_ref, parts, extra):
    got = multiply(basis_ref[...], parts[...].reshape(basis_ref.shape[1], parts.shape[2]))
    cases = got.shape[1] // 2
    rows = got[:ROWS, :cases] + got[:ROWS, cases:] + got[ROWS:, :cases]
    index = lax.broadcasted_iota(jnp.int32, rows.shape, 0)
    for k, row in enumerate(extra):
        rows = jnp.where(index == NEAR - 4 + k, row, rows)
    for copy in range(out_ref.shape[0]):
        out_ref[copy] = rows
    return rows


def column_sum(value):
    return jnp.sum(value, axis=0, keepdims=True)


def wide_body(me, corner, coarse, out):
    block = coarse.shape[0]
    count = out.shape[0]
    lane = lax.broadcasted_iota(jnp.int32, (block, out.shape[2] - block), 1)
    spare = jnp.where(lane == 2 * me[0], corner[0, 0], 0) + jnp.where(lane == 2 * me[0] + 1, corner[1, 0], 0)
    wide = jnp.concatenate([coarse[...], spare.astype(F32)], 1)
    for copy in range(count):
        out[copy] = wide


def begin_body(count, corner, rhs, scaling, basis, east, above, places, coarse, blocks, *refs):
    res, east0, north0, north1, gain, edges, message, parts, tiles, moved = refs
    side, cases = rhs.shape[1], rhs.shape[2]
    copies = [
        pltpu.make_async_copy(blocks.at[4 * s, pl.ds(0, cases), pl.ds(0, cases)], tiles.at[s], moved.at[s])
        for s in range(2)
    ]
    for copy in copies:
        copy.start()
    high, low = split(scaling[...])
    least = (scaling[...] - high.astype(F32) - low.astype(F32)).astype(BF16)
    thirds = jnp.concatenate([high.astype(F32), low.astype(F32), least.astype(F32)], 0).astype(BF16)
    row = lax.broadcasted_iota(jnp.int32, (12, cases), 0)
    norm = jnp.zeros((1, cases), F32)
    for edge in range(4):
        s, e = divmod(edge, 2)
        index = lax.broadcasted_iota(jnp.int32, (side, cases), 0)
        mask = index < count[s, e]
        chosen = (row % 4 == edge).astype(F32).astype(BF16)
        wide = lax.dot_general(thirds, chosen, (((0,), (0,)), ((), ())), preferred_element_type=F32)
        gain[edge] = jnp.where(mask, wide, 0.0)
        res[edge] = jnp.where(mask, rhs[edge], 0.0)
        value = gain[edge] * res[edge]
        norm = norm + column_sum(res[edge] * value)
        put_edge(edge, value, east0, north0, north1, parts)
        own = basis[s, :, 2 * e * side : (2 * e + 1) * side].astype(BF16)
        if e == 0:
            other = east[s].astype(BF16)
        elif s == 0:
            other = basis[1, :, 3 * side :].astype(BF16)
        else:
            other = above[...].astype(BF16)
        place = places[edge].astype(BF16)
        value = multiply(place[:, : 4 * CS], own) + multiply(place[:, 16 : 16 + 4 * CS], other)
        high, low = split(value)
        edges[:ROWS, edge * side : (edge + 1) * side] = high
        edges[ROWS:, edge * side : (edge + 1) * side] = low
    for ref in (east0, north1, north0, res, gain, edges):
        ref.send()
    lane = lax.broadcasted_iota(jnp.int32, (1, cases), 1)
    numbers = jnp.where(lane == 0, corner[0, 0], 0) + jnp.where(lane == 1, corner[1, 0], 0)
    index = lax.broadcasted_iota(jnp.int32, (cases, cases), 0)
    diagonal = index == lax.broadcasted_iota(jnp.int32, (cases, cases), 1)
    size = jnp.zeros((1, cases), F32)
    for s in range(2):
        copies[s].wait()
        tile = tiles[s].astype(F32)
        size = size + jnp.sum(jnp.where(diagonal, tile, 0.0)) / (512.0 * cases)
    size = size + jnp.sum(jnp.abs(coarse[...])) / (16.0 * coarse.shape[0])
    message_to(message, edges, parts, [norm, numbers.astype(F32), size])


def put_edge(edge, value, east, north0, north1, parts):
    side = value.shape[0]
    if edge % 2 == 0:
        east[edge // 2] = value
    elif edge == 1:
        north0[...] = value
    else:
        north1[...] = value
    high, low = split(value)
    parts[edge, :, : value.shape[1]] = high
    parts[edge, :, value.shape[1] :] = low


def apply_rows(block, parts):
    out = multiply(block, parts)
    cases = out.shape[1] // 2
    return out[:, :cases] + out[:, cases:]


def fetch(source, held, arrived, wanted):
    copies = [pltpu.make_async_copy(source.at[k], held.at[n], arrived.at[n]) for n, k in enumerate(wanted)]
    for copy in copies:
        copy.start()
    return copies


def weighed(parts, s, q, out):
    side, cases = out.shape
    rows = parts[s, q * side : (q + 1) * side]
    return column_sum((rows[:, :cases].astype(F32) + rows[:, cases:].astype(F32)) * out)


GIVEN = (1, 5, 3)


def give_body(own_east, own_north0, own_north1, west, below, blocks, out_east, out_north, parts, product, held, arrived):
    copies = fetch(blocks, held, arrived, GIVEN)
    side = west.shape[1]
    for s in range(2):
        parts[s, side : 2 * side] = halves(-west[s])
    parts[0, 3 * side :] = halves(-below[...])
    for s in range(2):
        parts[s, :side] = halves(own_east[s])
    parts[0, 2 * side : 3 * side] = halves(own_north0[...])
    parts[1, 3 * side :] = halves(-own_north0[...])
    parts[1, 2 * side : 3 * side] = halves(own_north1[...])
    total = 0.0
    for n, (s, q) in enumerate([(0, 1), (1, 1), (0, 3)]):
        copies[n].wait()
        value = apply_rows(held[n], parts[s])
        if n < 2:
            out_east[s] = value
        else:
            out_north[...] = value
        if n == 1:
            out_east.send()
        total = total + weighed(parts, s, q, value)
    product[...] = jnp.broadcast_to(total, product.shape)


def keep_body(parts, product_in, blocks, out, product, held, arrived):
    copies = fetch(blocks, held, arrived, (0, 2, 7, 4, 6))
    total = product_in[0:1]
    for n, (edge, s, q) in enumerate([(0, 0, 0), (1, 0, 2), (1, 1, 3), (2, 1, 0), (3, 1, 2)]):
        copies[n].wait()
        value = apply_rows(held[n], parts[s])
        total = total + weighed(parts, s, q, value)
        out[edge] = out[edge] - value if n == 2 else value
    product[...] = jnp.broadcast_to(total, product.shape)


def sum_body(product, rows, got, out):
    total = got[0]
    for k in range(1, got.shape[0]):
        total = total + got[k]
    index = lax.broadcasted_iota(jnp.int32, total.shape, 0) % NEAR
    value = product[0:1] + column_sum(jnp.where(index < 4 * CS, rows[...] * total, 0.0))
    out[...] = jnp.broadcast_to(value, out.shape)


def arrange_body(lanes, below, own, beyond, *outs):
    lane = lanes[...].astype(BF16)
    width = lane.shape[1]
    for ii, source in enumerate([below, own, beyond]):
        high, low = split(source[...])
        high = multiply(high, lane).astype(BF16)
        low = multiply(low, lane).astype(BF16)
        outs[0][:, ii * width : (ii + 1) * width] = high
        outs[1][:, ii * width : (ii + 1) * width] = low


def row_pieces(same, other, ii):
    return [ref[z, ii * NEAR : (ii + 1) * NEAR] for ref in (same, other) for z in range(same.shape[0])]


def lay_out(value, first, out):
    gx, cases = out.shape[0], out.shape[2]
    total = first[0][NEAR - 8 :]
    for piece in first[1:]:
        total = total + piece[NEAR - 8 :]
    index = lax.broadcasted_iota(jnp.int32, (8, cases), 0)
    for target in range(gx):
        for ii in range(3):
            at = ((target - 1 + ii) % gx) * NEAR
            out[target, ii * NEAR : ii * NEAR + 8] = value[at : at + 8]
            rest = value[at + 8 : at + 16]
            if ii == 0:
                rest = jnp.where(index < 4, rest, total)
            out[target, ii * NEAR + 8 : ii * NEAR + 16] = rest


def coarse_body(high, low, same, other, out):
    cases = same.shape[2]
    pieces = [row_pieces(same, other, ii) for ii in range(3)]
    gathered = halves(jnp.concatenate(pieces[0] + pieces[1] + pieces[2], 0))
    product = multiply(high[...], gathered)
    value = product[:, :cases] + product[:, cases:] + multiply(low[...], gathered[:, :cases])
    lay_out(value, pieces[0], out)


def first_coarse_body(lanes, own, same, other, lower, upper, out):
    cases = same.shape[2]
    lane = lanes[...].astype(BF16)
    high, low = split(own[...])
    high = multiply(high, lane).astype(BF16)
    low = multiply(low, lane).astype(BF16)
    middle = row_pieces(same, other, 1)
    half = same.shape[0]
    pieces = [
        middle[k] + lower[k // half, k % half] + upper[k // half, k % half] for k in range(2 * half)
    ]
    gathered = halves(jnp.concatenate(pieces, 0))
    product = multiply(high, gathered)
    value = product[:, :cases] + product[:, cases:] + multiply(low, gathered[:, :cases])
    lay_out(value, row_pieces(same, other, 0), out)


def image_body(last, part, east, north, got, edges, gain, *refs):
    side, cases = part.shape[1], part.shape[2]
    if last:
        u_ref, spare = refs
    else:
        (prev_east, prev_north0, prev_north1), refs = refs[:3], refs[3:]
        kappa_in, refs = (refs[0], refs[1:]) if len(refs) == 10 else (None, refs)
        u_ref, w_east, w_north0, w_north1, kappa_out, spare, rows_out, message, own = refs
    total = got[0]
    for k in range(1, got.shape[0]):
        total = total + got[k]
    high, low = split(total)
    twice = jnp.concatenate(
        [jnp.concatenate([high, low], 1), jnp.concatenate([high, jnp.zeros_like(low)], 1)], 0
    )
    spare[...] = total[NEAR - 8 : NEAR]
    if not last:
        kappa = 4.0 / total[NEAR - 2 : NEAR - 1] if kappa_in is None else kappa_in[0:1]
        kappa_out[...] = jnp.broadcast_to(kappa, kappa_out.shape)
    first = jnp.zeros((1, cases), F32)
    second = jnp.zeros((1, cases), F32)
    for edge in (1, 3, 0, 2):
        coarse = lax.dot_general(
            edges[:, edge * side : (edge + 1) * side],
            twice,
            (((0,), (0,)), ((), ())),
            preferred_element_type=F32,
        )
        value = part[edge] + coarse[:, :cases] + coarse[:, cases:]
        if edge % 2 == 0:
            value = value - east[edge // 2]
        elif edge == 3:
            value = value - north[...]
        image = jnp.where(gain[edge] > 0.0, value, 0.0)
        u_ref[edge] = image
        if not last:
            previous = (prev_north0, prev_north1)[edge // 2][...] if edge % 2 else prev_east[edge // 2]
            first = first + column_sum(previous * image)
            following = kappa * gain[edge] * value
            second = second + column_sum(following * image)
            put_edge(edge, following, w_east, w_north0, w_north1, own)
    if last:
        return
    for ref in (w_east, w_north1, w_north0, u_ref):
        ref.send()
    rows_out[...] = message_to(message, edges, own, [first, second])


def image_call(part, east, north, got, edges, gain, previous, kappa, copies):
    _, side, cases = part.shape
    shape = lambda *dims: jax.ShapeDtypeStruct(dims + (cases,), F32)
    outs = (
        shape(4, side),
        shape(2, side),
        shape(side),
        shape(side),
        shape(8),
        shape(8),
        shape(ROWS),
        shape(copies, ROWS),
    )
    operands = (part, east, north, got, edges, gain, *previous) + (() if kappa is None else (kappa,))
    return kernel_call(
        functools.partial(image_body, False),
        outs,
        operands,
        scratch=(pltpu.VMEM((4, side, 2 * cases), BF16),),
        fast=range(4),
    )


def slot_of(source, core, half):
    return source // 2 + half * ((source + core) % 2)


def pick_body(numbers, me, columns, out, rows):
    half = numbers.shape[0] // 2
    block = out.shape[1]
    rows[...] = jnp.zeros_like(rows)
    core = me[1] % 2
    for j in range(4 * half):
        node = numbers[slot_of(j // 2, core, half), j % 2]
        for c in range(CS):
            at = node * CS + c
            rows[pl.ds(j * CS + c, 1)] = columns[pl.ds(at // block, 1), pl.ds(at % block, 1)].reshape(1, -1)
    turned = rows[...].T[:block]
    known = jnp.zeros((1, turned.shape[1]), F32)
    for k in range(columns.shape[0]):
        known = known + columns[k, :1]
    lane = lax.broadcasted_iota(jnp.int32, turned.shape, 1)
    turned = jnp.where(lane >= block, known, turned)
    for copy in range(half):
        out[copy] = turned


def near_body(gx, numbers, me, same, other, out):
    half = same.shape[0]
    block = same.shape[1]
    out[...] = jnp.zeros(out.shape, F32)
    core = me[1] % 2
    lane = lax.broadcasted_iota(jnp.int32, (1, same.shape[2]), 1)
    for jj in range(4):
        j = (2 * me[1] - 1 + jj + 4 * half) % (4 * half)
        slot = slot_of(j // 2, core, half)
        for i in range(gx):
            node = numbers[slot, block + 2 * i + j % 2]
            owner = node * CS // block
            row = node * CS - owner * block
            mine = owner % 2 == core
            for c in range(CS):
                first = same[pl.ds(owner // 2, 1), pl.ds(row + c, 1)].reshape(1, -1)
                second = other[pl.ds(owner // 2, 1), pl.ds(row + c, 1)].reshape(1, -1)
                value = jnp.where(mine, first, second)
                out[pl.ds(i * NEAR + jj * CS + c, 1)] = jnp.where(lane < block, value, 0.0)


def finish_body(kappa_ref, spare0, spare1, spare2, last, *refs):
    (res, *fields), (u1, u2, u3, mult_out, res_out) = refs[:10], refs[10:]
    kappa = kappa_ref[0:1]
    moments = [
        spare0[4:5],
        kappa * spare1[4:5],
        kappa * spare1[5:6],
        kappa * spare2[4:5],
        kappa * spare2[5:6],
        kappa * column_sum(last[...]),
    ]

    def form(first, second, shift):
        total = 0.0
        for i, x in enumerate(first):
            for j, y in enumerate(second):
                total = total + x * y * moments[i + j + shift]
        return total

    one = jnp.ones_like(kappa)
    rho, pi, gamma = [one], [one], []
    rz = moments[0]
    for iteration in range(3):
        step = rz / form(pi, pi, 1)
        gamma = [(gamma[k] if k < len(gamma) else 0.0) + step * pi[k] for k in range(len(pi))]
        rho = [one] + [-value for value in gamma]
        if iteration < 2:
            rz_new = form(rho, rho, 0)
            ratio = rz_new / rz
            pi = [rho[k] + (ratio * pi[k] if k < len(pi) else 0.0) for k in range(len(rho))]
            rz = rz_new
    gamma = [kappa * value for value in gamma]
    for edge in range(4):
        total = 0.0
        for k in range(3):
            east, north0, north1 = fields[3 * k : 3 * k + 3]
            value = east[edge // 2] if edge % 2 == 0 else (north0, north1)[edge // 2][...]
            total = total + gamma[k] * value
        mult_out[edge] = total
    mult_out.send()
    for edge in range(4):
        res_out[edge] = res[edge] - (gamma[0] * u1[edge] + gamma[1] * u2[edge] + gamma[2] * u3[edge])


def local(dual_rhs, scaling, dual_count, corner_map, local_ops, corner_basis, coarse_inverse):
    gx, gy = lax.axis_size("sx"), lax.axis_size("sy")
    a, b = lax.axis_index("sx"), lax.axis_index("sy")
    side, cases = dual_rhs.shape[3], dual_rhs.shape[4]
    rhs = dual_rhs.reshape(4, side, cases)
    blocks = local_ops.reshape(8, side, 4 * side)
    block = coarse_inverse.shape[0]
    half = gy // 2
    basis = corner_basis[0]
    me = jnp.stack([a, b]).astype(jnp.int32)
    shape = lambda *dims: jax.ShapeDtypeStruct(dims + (cases,), F32)
    field = shape(4, side)
    double = lambda *dims: jax.ShapeDtypeStruct(dims + (2 * cases,), BF16)
    wide = kernel_call(wide_body, shape(gx, block), (me, corner_map[0], coarse_inverse), 2)
    columns_all = lax.all_to_all(wide, "sx", 0, 0, tiled=True)
    wide_basis = basis.astype(F32)
    east = shifted(wide_basis[:, :, side : 2 * side], "sx", -1)
    above = shifted(wide_basis[0, :, 3 * side :], "sy", -1)

    residual, *w0, gain, edges, message = kernel_call(
        begin_body,
        (
            field,
            shape(2, side),
            shape(side),
            shape(side),
            field,
            jax.ShapeDtypeStruct((2 * ROWS, 4 * side), BF16),
            shape(half, ROWS),
        ),
        (
            dual_count[0],
            corner_map[0],
            rhs,
            scaling.reshape(4, side),
            wide_basis,
            east,
            above,
            jnp.asarray(place_matrices()),
            coarse_inverse,
        ),
        2,
        raw=(blocks,),
        scratch=(
            pltpu.VMEM((4, side, 2 * cases), BF16),
            pltpu.VMEM((2, cases, cases), BF16),
            pltpu.SemaphoreType.DMA((2,)),
        ),
        fast=(4, 5, 6),
    )
    message, columns_all = lax.optimization_barrier((message, columns_all))

    def halo(vector):
        return shifted(vector[0], "sx", 1), shifted(vector[2], "sy", 1)

    def held(count):
        return (pltpu.VMEM((count,) + blocks.shape[1:], BF16), pltpu.SemaphoreType.DMA((count,)))

    def give(own, west, below):
        given_east, given_north, parts, product = kernel_call(
            give_body,
            (shape(2, side), shape(side), double(2, 4 * side), shape(8)),
            (*own, west, below),
            raw=(blocks,),
            scratch=held(3),
            fast=(3, 4),
            fast_outs=(2,),
        )
        return (parts, product), shifted(given_east, "sx", -1), shifted(given_north, "sy", -1)

    def keep(given):
        return kernel_call(
            keep_body, (field, shape(8)), given, raw=(blocks,), scratch=held(5), fast=(0,), fast_outs=(0,)
        )

    west, below = halo(w0)
    same, other = along_sy(message)
    lower = shifted(jnp.stack([same[:, :NEAR], other[:, :NEAR]]), "sx", -1)
    upper = shifted(jnp.stack([same[:, 2 * NEAR :], other[:, 2 * NEAR :]]), "sx", 1)
    numbers = jnp.concatenate([same[:, NEAR - 3], other[:, NEAR - 3]], 0).astype(jnp.int32)
    turned = kernel_call(
        pick_body,
        shape(half, block),
        (numbers, me, columns_all),
        2,
        scratch=(pltpu.VMEM((cases, cases), F32),),
        fast=(2,),
    )
    turned, west, below = lax.optimization_barrier((turned, west, below))
    given, back_east, back_north = give(w0, west, below)
    kept, _ = keep(given)
    rows_same, rows_other, (kept, lower, upper) = along_sy(turned, (kept, lower, upper))
    numbers = jnp.concatenate([rows_same[:, 0], rows_other[:, 0]], 0).astype(jnp.int32)
    own_part = kernel_call(
        functools.partial(near_body, gx),
        shape(gx * NEAR),
        (numbers, me, rows_same, rows_other),
        2,
        fast=(2, 3),
    )
    below_part = shifted(own_part, "sx", 1)
    beyond_part = shifted(own_part, "sx", -1)
    lanes = lax.dynamic_index_in_dim(jnp.asarray(lane_matrices(gy)), b % 2, 0, keepdims=False)

    send = kernel_call(
        first_coarse_body,
        shape(gx, ROWS),
        (lanes, own_part, same, other, lower, upper),
        fast=range(2, 6),
    )
    got = lax.all_to_all(send, "sx", 0, 0, tiled=True)
    u1, *w1, kappa, spare0, _, message = image_call(
        kept, back_east, back_north, got, edges, gain, w0, None, half
    )
    w_shape = jax.ShapeDtypeStruct((gx * NEAR, ROWS * gy), BF16)
    high, low = kernel_call(
        arrange_body, (w_shape, w_shape), (lanes, below_part, own_part, beyond_part), fast=(1, 3)
    )

    def coarse_solve(same, other):
        send = kernel_call(coarse_body, shape(gx, ROWS), (high, low, same, other), fast=(2, 3))
        return lax.all_to_all(send, "sx", 0, 0, tiled=True)

    west, below = halo(w1)
    same, other = along_sy(message)
    given, back_east, back_north = give(w1, west, below)
    got = coarse_solve(same, other)
    kept, _ = keep(given)
    u2, *w2, _, spare1, rows, message = image_call(
        kept, back_east, back_north, got, edges, gain, w1, kappa, half
    )
    west, below = halo(w2)
    same, other = along_sy(message)
    given, back_east, back_north = give(w2, west, below)
    got = coarse_solve(same, other)
    kept, product = keep(given)
    last = kernel_call(sum_body, shape(gx * gy), (product, rows, got), fast=(2,))
    last = lax.all_to_all(last.reshape(gx * gy, 1, cases), ("sx", "sy"), 0, 0, tiled=True)
    u3, spare2 = kernel_call(
        functools.partial(image_body, True),
        (field, shape(8)),
        (kept, back_east, back_north, got, edges, gain),
        fast=range(4),
    )
    multipliers, residual = kernel_call(
        finish_body,
        (field, field),
        (
            kappa,
            spare0,
            spare1,
            spare2,
            last.reshape(gx * gy, cases),
            residual,
            *w0,
            *w1,
            *w2,
            u1,
            u2,
            u3,
        ),
        fast=(4,),
    )
    return multipliers.reshape(dual_rhs.shape), residual.reshape(dual_rhs.shape)


def solution(mesh):
    in_specs = (
        P("sx", "sy", None, None, None),
        P("sx", "sy", None, None),
        P("sx", "sy", None),
        P("sx", "sy", None),
        P("sx", "sy", None, None),
        P("sx", "sy", None, None),
        P("sx", "sy"),
    )
    out_specs = (P("sx", "sy", None, None, None), P("sx", "sy", None, None, None))
    return jax.shard_map(local, mesh=mesh, in_specs=in_specs, out_specs=out_specs, check_vma=False)
```

```python
import functools
import math

import numpy as np
import jax
import jax.numpy as jnp
from jax import lax
from jax.experimental import pallas as pl
from jax.experimental.pallas import tpu as pltpu
from jax.sharding import PartitionSpec as P

CS = 3
NEAR = 16
ROWS = 3 * NEAR
F32, BF16 = jnp.float32, jnp.bfloat16
SMEM = pl.BlockSpec(memory_space=pltpu.SMEM)


def shifted(array, axis, by):
    count = lax.axis_size(axis)
    return lax.ppermute(array, axis, [(i, (i + by) % count) for i in range(count)])


def along_sy(copies, beside=None):
    count = lax.axis_size("sy")
    groups = [[2 * z + core for z in range(count // 2)] for core in range(2)]
    same = lax.all_to_all(copies, "sy", 0, 0, tiled=True, axis_index_groups=groups)
    if beside is not None:
        same, beside = lax.optimization_barrier((same, beside))
    other = lax.ppermute(same, "sy", [(i, i ^ 1) for i in range(count)])
    return (same, other) if beside is None else (same, other, beside)


class Arriving:
    def __init__(self, source, held, arrived):
        self.copy = pltpu.make_async_copy(source, held, arrived)
        self.copy.start()
        self.held, self.shape, self.waiting = held, held.shape, True

    def settle(self):
        if self.waiting:
            self.copy.wait()
        self.waiting = False

    def __getitem__(self, index):
        self.settle()
        return self.held[index]


class Leaving:
    def __init__(self, held, target, arrived):
        self.copy = pltpu.make_async_copy(held, target, arrived)
        self.held, self.shape, self.sent = held, held.shape, False

    def __getitem__(self, index):
        return self.held[index]

    def __setitem__(self, index, value):
        self.held[index] = value

    def send(self):
        if not self.sent:
            self.copy.start()
        self.sent = True


def kernel_call(body, outs, operands, scalars=0, raw=(), scratch=(), fast=(), fast_outs=()):
    several = isinstance(outs, tuple)
    outs = outs if several else (outs,)
    operands = tuple(operands)
    count_in, count_out = len(operands), len(outs)
    slow_in = [k for k in range(scalars, count_in) if k not in fast]
    slow_out = [k for k in range(count_out) if k not in fast_outs]
    held = [pltpu.VMEM(operands[k].shape, operands[k].dtype) for k in slow_in]
    held += [pltpu.VMEM(outs[k].shape, outs[k].dtype) for k in slow_out]
    arrays = list(operands) + list(raw)
    moved = sum(4 * math.prod(array.shape) for array in arrays + list(outs))

    def wrapped(*refs):
        refs = list(refs)
        ins, refs = refs[: len(arrays)], refs[len(arrays) :]
        results, refs = refs[:count_out], refs[count_out:]
        buffers, refs = refs[: len(held)], refs[len(held) :]
        arrived, extra = refs[0], refs[1:]
        for n, k in enumerate(slow_in):
            ins[k] = Arriving(ins[k], buffers[n], arrived.at[n])
        for n, k in enumerate(slow_out, len(slow_in)):
            results[k] = Leaving(buffers[n], results[k], arrived.at[n])
        body(*ins, *results, *extra)
        for k in slow_in:
            ins[k].settle()
        for k in slow_out:
            results[k].send()
        for k in slow_out:
            results[k].copy.wait()

    def spec(k):
        return SMEM if k < scalars else pl.BlockSpec(memory_space=pltpu.VMEM if k in fast else pltpu.HBM)

    arrays = [
        array if k < scalars or k in fast else pltpu.with_memory_space_constraint(array, pltpu.HBM)
        for k, array in enumerate(arrays)
    ]
    out_specs = tuple(
        pl.BlockSpec(memory_space=pltpu.VMEM if k in fast_outs else pltpu.HBM) for k in range(count_out)
    )
    out_shape = tuple(
        (pltpu.VMEM if k in fast_outs else pltpu.HBM)(array.shape, array.dtype) for k, array in enumerate(outs)
    )
    got = pl.pallas_call(
        wrapped,
        in_specs=[spec(k) for k in range(len(arrays))],
        out_specs=out_specs,
        out_shape=out_shape,
        scratch_shapes=held + [pltpu.SemaphoreType.DMA((max(len(held), 1),))] + list(scratch),
        compiler_params=pltpu.CompilerParams(vmem_limit_bytes=16 * 2**20),
        cost_estimate=pl.CostEstimate(flops=4 * moved, bytes_accessed=moved, transcendentals=0),
    )(*arrays)
    return tuple(got) if several else got[0]


def split(value):
    high = value.astype(BF16)
    return high, (value - high.astype(F32)).astype(BF16)


def halves(value):
    return jnp.concatenate(split(value), 1)


def multiply(first, second):
    return jnp.dot(first, second, preferred_element_type=F32)


def place_matrices():
    place = [(0, 0), (-1, 0), (0, -1), (-1, -1)]
    out = np.zeros((4, ROWS, 32), np.float32)
    for s in range(2):
        for e in range(2):
            for k, (di, dj) in enumerate(place):
                for c in range(CS):
                    out[2 * s + e, (1 + di) * NEAR + (1 + s + dj) * CS + c, k * CS + c] += 1
                    row = (1 + di + (1 - e)) * NEAR + (1 + s + dj + e) * CS + c
                    out[2 * s + e, row, 16 + k * CS + c] -= 1
    return out


def lane_matrices(gy):
    out = np.zeros((2, 128, gy * NEAR), np.float32)
    for core in range(2):
        for slot in range(gy):
            z, other = slot % (gy // 2), slot // (gy // 2)
            source = 2 * z + (core ^ other)
            for jj in range(4):
                for c in range(CS):
                    j = (2 * source - 1 + jj) % (2 * gy)
                    out[core, j * CS + c, slot * NEAR + jj * CS + c] = 1
    return out


def message_to(out_ref, basis_ref, parts, extra):
    got = multiply(basis_ref[...], parts[...].reshape(basis_ref.shape[1], parts.shape[2]))
    cases = got.shape[1] // 2
    rows = got[:ROWS, :cases] + got[:ROWS, cases:] + got[ROWS:, :cases]
    index = lax.broadcasted_iota(jnp.int32, rows.shape, 0)
    for k, row in enumerate(extra):
        rows = jnp.where(index == NEAR - 4 + k, row, rows)
    for copy in range(out_ref.shape[0]):
        out_ref[copy] = rows
    return rows


def column_sum(value):
    return jnp.sum(value, axis=0, keepdims=True)


def wide_body(me, corner, coarse, out):
    block = coarse.shape[0]
    count = out.shape[0]
    lane = lax.broadcasted_iota(jnp.int32, (block, out.shape[2] - block), 1)
    spare = jnp.where(lane == 2 * me[0], corner[0, 0], 0) + jnp.where(lane == 2 * me[0] + 1, corner[1, 0], 0)
    wide = jnp.concatenate([coarse[...], spare.astype(F32)], 1)
    for copy in range(count):
        out[copy] = wide


def begin_body(count, corner, rhs, scaling, basis, east, above, places, coarse, blocks, *refs):
    res, east0, north0, north1, gain, edges, message, parts, tiles, moved = refs
    side, cases = rhs.shape[1], rhs.shape[2]
    copies = [
        pltpu.make_async_copy(blocks.at[4 * s, pl.ds(0, cases), pl.ds(0, cases)], tiles.at[s], moved.at[s])
        for s in range(2)
    ]
    for copy in copies:
        copy.start()
    high, low = split(scaling[...])
    least = (scaling[...] - high.astype(F32) - low.astype(F32)).astype(BF16)
    thirds = jnp.concatenate([high.astype(F32), low.astype(F32), least.astype(F32)], 0).astype(BF16)
    row = lax.broadcasted_iota(jnp.int32, (12, cases), 0)
    norm = jnp.zeros((1, cases), F32)
    for edge in range(4):
        s, e = divmod(edge, 2)
        index = lax.broadcasted_iota(jnp.int32, (side, cases), 0)
        mask = index < count[s, e]
        chosen = (row % 4 == edge).astype(F32).astype(BF16)
        wide = lax.dot_general(thirds, chosen, (((0,), (0,)), ((), ())), preferred_element_type=F32)
        gain[edge] = jnp.where(mask, wide, 0.0)
        res[edge] = jnp.where(mask, rhs[edge], 0.0)
        value = gain[edge] * res[edge]
        norm = norm + column_sum(res[edge] * value)
        put_edge(edge, value, east0, north0, north1, parts)
        own = basis[s, :, 2 * e * side : (2 * e + 1) * side].astype(BF16)
        if e == 0:
            other = east[s].astype(BF16)
        elif s == 0:
            other = basis[1, :, 3 * side :].astype(BF16)
        else:
            other = above[...].astype(BF16)
        place = places[edge].astype(BF16)
        value = multiply(place[:, : 4 * CS], own) + multiply(place[:, 16 : 16 + 4 * CS], other)
        high, low = split(value)
        edges[:ROWS, edge * side : (edge + 1) * side] = high
        edges[ROWS:, edge * side : (edge + 1) * side] = low
    for ref in (east0, north1, north0, res, gain, edges):
        ref.send()
    lane = lax.broadcasted_iota(jnp.int32, (1, cases), 1)
    numbers = jnp.where(lane == 0, corner[0, 0], 0) + jnp.where(lane == 1, corner[1, 0], 0)
    index = lax.broadcasted_iota(jnp.int32, (cases, cases), 0)
    diagonal = index == lax.broadcasted_iota(jnp.int32, (cases, cases), 1)
    size = jnp.zeros((1, cases), F32)
    for s in range(2):
        copies[s].wait()
        tile = tiles[s].astype(F32)
        size = size + jnp.sum(jnp.where(diagonal, tile, 0.0)) / (512.0 * cases)
    size = size + jnp.sum(jnp.abs(coarse[...])) / (16.0 * coarse.shape[0])
    message_to(message, edges, parts, [norm, numbers.astype(F32), size])


def put_edge(edge, value, east, north0, north1, parts):
    side = value.shape[0]
    if edge % 2 == 0:
        east[edge // 2] = value
    elif edge == 1:
        north0[...] = value
    else:
        north1[...] = value
    high, low = split(value)
    parts[edge, :, : value.shape[1]] = high
    parts[edge, :, value.shape[1] :] = low


def apply_rows(block, parts):
    out = multiply(block, parts)
    cases = out.shape[1] // 2
    return out[:, :cases] + out[:, cases:]


def fetch(source, held, arrived, wanted):
    copies = [pltpu.make_async_copy(source.at[k], held.at[n], arrived.at[n]) for n, k in enumerate(wanted)]
    for copy in copies:
        copy.start()
    return copies


def weighed(parts, s, q, out):
    side, cases = out.shape
    rows = parts[s, q * side : (q + 1) * side]
    return column_sum((rows[:, :cases].astype(F32) + rows[:, cases:].astype(F32)) * out)


GIVEN = (1, 5, 3)


def give_body(weigh, own_east, own_north0, own_north1, west, below, blocks, out_east, out_north, parts, *refs):
    *product, held, arrived = refs
    copies = fetch(blocks, held, arrived, GIVEN)
    side = west.shape[1]
    for s in range(2):
        parts[s, side : 2 * side] = halves(-west[s])
    parts[0, 3 * side :] = halves(-below[...])
    for s in range(2):
        parts[s, :side] = halves(own_east[s])
    parts[0, 2 * side : 3 * side] = halves(own_north0[...])
    parts[1, 3 * side :] = halves(-own_north0[...])
    parts[1, 2 * side : 3 * side] = halves(own_north1[...])
    total = 0.0
    for n, (s, q) in enumerate([(0, 1), (1, 1), (0, 3)]):
        copies[n].wait()
        value = apply_rows(held[n], parts[s])
        if n < 2:
            out_east[s] = value
        else:
            out_north[...] = value
        if n == 1:
            out_east.send()
        if weigh:
            total = total + weighed(parts, s, q, value)
    if weigh:
        product[0][...] = jnp.broadcast_to(total, product[0].shape)


def keep_body(weigh, parts, *refs):
    if weigh:
        product_in, blocks, out, product, held, arrived = refs
    else:
        blocks, out, held, arrived = refs
    copies = fetch(blocks, held, arrived, (0, 2, 7, 4, 6))
    total = 0.0
    for n, (edge, s, q) in enumerate([(0, 0, 0), (1, 0, 2), (1, 1, 3), (2, 1, 0), (3, 1, 2)]):
        copies[n].wait()
        value = apply_rows(held[n], parts[s])
        if weigh:
            total = total + weighed(parts, s, q, value)
        out[edge] = out[edge] - value if n == 2 else value
    if weigh:
        product[...] = jnp.broadcast_to(product_in[0:1] + total, product.shape)


def sum_body(product, rows, got, out):
    total = got[0]
    for k in range(1, got.shape[0]):
        total = total + got[k]
    index = lax.broadcasted_iota(jnp.int32, total.shape, 0) % NEAR
    value = product[0:1] + column_sum(jnp.where(index < 4 * CS, rows[...] * total, 0.0))
    out[...] = jnp.broadcast_to(value, out.shape)


def row_pieces(same, other, ii):
    return [ref[z, ii * NEAR : (ii + 1) * NEAR] for ref in (same, other) for z in range(same.shape[0])]


def lay_out(value, first, out):
    gx, cases = out.shape[0], out.shape[2]
    total = first[0][NEAR - 8 :]
    for piece in first[1:]:
        total = total + piece[NEAR - 8 :]
    index = lax.broadcasted_iota(jnp.int32, (8, cases), 0)
    for target in range(gx):
        for ii in range(3):
            at = ((target - 1 + ii) % gx) * NEAR
            out[target, ii * NEAR : ii * NEAR + 8] = value[at : at + 8]
            rest = value[at + 8 : at + 16]
            if ii == 0:
                rest = jnp.where(index < 4, rest, total)
            out[target, ii * NEAR + 8 : ii * NEAR + 16] = rest


def laid(source, lane):
    return tuple(multiply(part, lane).astype(BF16) for part in split(source[...]))


def coarse_body(lanes, below, own, beyond, same, other, out):
    cases = same.shape[2]
    lane = lanes[...].astype(BF16)
    value = 0.0
    for ii, source in enumerate((own, below, beyond)):
        gathered = halves(jnp.concatenate(row_pieces(same, other, (1, 0, 2)[ii]), 0))
        high, low = laid(source, lane)
        product = multiply(high, gathered)
        value = value + product[:, :cases] + product[:, cases:] + multiply(low, gathered[:, :cases])
    lay_out(value, row_pieces(same, other, 0), out)


def first_coarse_body(lanes, own, same, other, lower, upper, out):
    cases = same.shape[2]
    high, low = laid(own, lanes[...].astype(BF16))
    middle = row_pieces(same, other, 1)
    half = same.shape[0]
    pieces = [
        middle[k] + lower[k // half, k % half] + upper[k // half, k % half] for k in range(2 * half)
    ]
    gathered = halves(jnp.concatenate(pieces, 0))
    product = multiply(high, gathered)
    value = product[:, :cases] + product[:, cases:] + multiply(low, gathered[:, :cases])
    lay_out(value, row_pieces(same, other, 0), out)


def image_body(last, part, east, north, got, edges, gain, *refs):
    side, cases = part.shape[1], part.shape[2]
    if last:
        u_ref, spare = refs
    else:
        (prev_east, prev_north0, prev_north1), refs = refs[:3], refs[3:]
        kappa_in, refs = (refs[0], refs[1:]) if len(refs) == 10 else (None, refs)
        u_ref, w_east, w_north0, w_north1, kappa_out, spare, rows_out, message, own = refs
    total = got[0]
    for k in range(1, got.shape[0]):
        total = total + got[k]
    high, low = split(total)
    twice = jnp.concatenate(
        [jnp.concatenate([high, low], 1), jnp.concatenate([high, jnp.zeros_like(low)], 1)], 0
    )
    spare[...] = total[NEAR - 8 : NEAR]
    if not last:
        kappa = 4.0 / total[NEAR - 2 : NEAR - 1] if kappa_in is None else kappa_in[0:1]
        kappa_out[...] = jnp.broadcast_to(kappa, kappa_out.shape)
    first = jnp.zeros((1, cases), F32)
    second = jnp.zeros((1, cases), F32)
    for edge in (1, 3, 0, 2):
        coarse = lax.dot_general(
            edges[:, edge * side : (edge + 1) * side],
            twice,
            (((0,), (0,)), ((), ())),
            preferred_element_type=F32,
        )
        value = part[edge] + coarse[:, :cases] + coarse[:, cases:]
        if edge % 2 == 0:
            value = value - east[edge // 2]
        elif edge == 3:
            value = value - north[...]
        image = jnp.where(gain[edge] > 0.0, value, 0.0)
        u_ref[edge] = image
        if not last:
            previous = (prev_north0, prev_north1)[edge // 2][...] if edge % 2 else prev_east[edge // 2]
            first = first + column_sum(previous * image)
            following = kappa * gain[edge] * value
            second = second + column_sum(following * image)
            put_edge(edge, following, w_east, w_north0, w_north1, own)
    if last:
        return
    for ref in (w_east, w_north1, w_north0, u_ref):
        ref.send()
    rows_out[...] = message_to(message, edges, own, [first, second])


def image_call(part, east, north, got, edges, gain, previous, kappa, copies):
    _, side, cases = part.shape
    shape = lambda *dims: jax.ShapeDtypeStruct(dims + (cases,), F32)
    outs = (
        shape(4, side),
        shape(2, side),
        shape(side),
        shape(side),
        shape(8),
        shape(8),
        shape(ROWS),
        shape(copies, ROWS),
    )
    operands = (part, east, north, got, edges, gain, *previous) + (() if kappa is None else (kappa,))
    return kernel_call(
        functools.partial(image_body, False),
        outs,
        operands,
        scratch=(pltpu.VMEM((4, side, 2 * cases), BF16),),
        fast=range(4),
    )


def slot_of(source, core, half):
    return source // 2 + half * ((source + core) % 2)


def pick_body(numbers, me, columns, out, rows):
    half = numbers.shape[0] // 2
    block = out.shape[1]
    rows[...] = jnp.zeros_like(rows)
    core = me[1] % 2
    for j in range(4 * half):
        node = numbers[slot_of(j // 2, core, half), j % 2]
        for c in range(CS):
            at = node * CS + c
            rows[pl.ds(j * CS + c, 1)] = columns[pl.ds(at // block, 1), pl.ds(at % block, 1)].reshape(1, -1)
    turned = rows[...].T[:block]
    known = jnp.zeros((1, turned.shape[1]), F32)
    for k in range(columns.shape[0]):
        known = known + columns[k, :1]
    lane = lax.broadcasted_iota(jnp.int32, turned.shape, 1)
    turned = jnp.where(lane >= block, known, turned)
    for copy in range(half):
        out[copy] = turned


def near_body(gx, numbers, me, same, other, out):
    half = same.shape[0]
    block = same.shape[1]
    out[...] = jnp.zeros(out.shape, F32)
    core = me[1] % 2
    lane = lax.broadcasted_iota(jnp.int32, (1, same.shape[2]), 1)
    for jj in range(4):
        j = (2 * me[1] - 1 + jj + 4 * half) % (4 * half)
        slot = slot_of(j // 2, core, half)
        for i in range(gx):
            node = numbers[slot, block + 2 * i + j % 2]
            owner = node * CS // block
            row = node * CS - owner * block
            mine = owner % 2 == core
            for c in range(CS):
                first = same[pl.ds(owner // 2, 1), pl.ds(row + c, 1)].reshape(1, -1)
                second = other[pl.ds(owner // 2, 1), pl.ds(row + c, 1)].reshape(1, -1)
                value = jnp.where(mine, first, second)
                out[pl.ds(i * NEAR + jj * CS + c, 1)] = jnp.where(lane < block, value, 0.0)


def finish_body(kappa_ref, spare0, spare1, spare2, last, *refs):
    (res, *fields), (u1, u2, u3, mult_out, res_out) = refs[:10], refs[10:]
    kappa = kappa_ref[0:1]
    moments = [
        spare0[4:5],
        kappa * spare1[4:5],
        kappa * spare1[5:6],
        kappa * spare2[4:5],
        kappa * spare2[5:6],
        kappa * column_sum(last[...]),
    ]

    def form(first, second, shift):
        total = 0.0
        for i, x in enumerate(first):
            for j, y in enumerate(second):
                total = total + x * y * moments[i + j + shift]
        return total

    one = jnp.ones_like(kappa)
    rho, pi, gamma = [one], [one], []
    rz = moments[0]
    for iteration in range(3):
        step = rz / form(pi, pi, 1)
        gamma = [(gamma[k] if k < len(gamma) else 0.0) + step * pi[k] for k in range(len(pi))]
        rho = [one] + [-value for value in gamma]
        if iteration < 2:
            rz_new = form(rho, rho, 0)
            ratio = rz_new / rz
            pi = [rho[k] + (ratio * pi[k] if k < len(pi) else 0.0) for k in range(len(rho))]
            rz = rz_new
    gamma = [kappa * value for value in gamma]
    for edge in range(4):
        total = 0.0
        for k in range(3):
            east, north0, north1 = fields[3 * k : 3 * k + 3]
            value = east[edge // 2] if edge % 2 == 0 else (north0, north1)[edge // 2][...]
            total = total + gamma[k] * value
        mult_out[edge] = total
    mult_out.send()
    for edge in range(4):
        res_out[edge] = res[edge] - (gamma[0] * u1[edge] + gamma[1] * u2[edge] + gamma[2] * u3[edge])


def local(dual_rhs, scaling, dual_count, corner_map, local_ops, corner_basis, coarse_inverse):
    gx, gy = lax.axis_size("sx"), lax.axis_size("sy")
    a, b = lax.axis_index("sx"), lax.axis_index("sy")
    side, cases = dual_rhs.shape[3], dual_rhs.shape[4]
    rhs = dual_rhs.reshape(4, side, cases)
    blocks = local_ops.reshape(8, side, 4 * side)
    block = coarse_inverse.shape[0]
    half = gy // 2
    basis = corner_basis[0]
    me = jnp.stack([a, b]).astype(jnp.int32)
    shape = lambda *dims: jax.ShapeDtypeStruct(dims + (cases,), F32)
    field = shape(4, side)
    double = lambda *dims: jax.ShapeDtypeStruct(dims + (2 * cases,), BF16)
    wide = kernel_call(wide_body, shape(gx, block), (me, corner_map[0], coarse_inverse), 2)
    columns_all = lax.all_to_all(wide, "sx", 0, 0, tiled=True)
    wide_basis = basis.astype(F32)
    east = shifted(wide_basis[:, :, side : 2 * side], "sx", -1)
    above = shifted(wide_basis[0, :, 3 * side :], "sy", -1)

    residual, *w0, gain, edges, message = kernel_call(
        begin_body,
        (
            field,
            shape(2, side),
            shape(side),
            shape(side),
            field,
            jax.ShapeDtypeStruct((2 * ROWS, 4 * side), BF16),
            shape(half, ROWS),
        ),
        (
            dual_count[0],
            corner_map[0],
            rhs,
            scaling.reshape(4, side),
            wide_basis,
            east,
            above,
            jnp.asarray(place_matrices()),
            coarse_inverse,
        ),
        2,
        raw=(blocks,),
        scratch=(
            pltpu.VMEM((4, side, 2 * cases), BF16),
            pltpu.VMEM((2, cases, cases), BF16),
            pltpu.SemaphoreType.DMA((2,)),
        ),
        fast=(4, 5, 6),
    )
    message, columns_all = lax.optimization_barrier((message, columns_all))

    def halo(vector):
        return shifted(vector[0], "sx", 1), shifted(vector[2], "sy", 1)

    def held(count):
        return (pltpu.VMEM((count,) + blocks.shape[1:], BF16), pltpu.SemaphoreType.DMA((count,)))

    def give(own, west, below, weigh=False):
        given_east, given_north, *given = kernel_call(
            functools.partial(give_body, weigh),
            (shape(2, side), shape(side), double(2, 4 * side)) + ((shape(8),) if weigh else ()),
            (*own, west, below),
            raw=(blocks,),
            scratch=held(3),
            fast=(3, 4),
            fast_outs=(2, 3),
        )
        return given, shifted(given_east, "sx", -1), shifted(given_north, "sy", -1)

    def keep(given, weigh=False):
        return kernel_call(
            functools.partial(keep_body, weigh),
            (field, shape(8)) if weigh else (field,),
            given,
            raw=(blocks,),
            scratch=held(5),
            fast=range(len(given)),
            fast_outs=(0, 1),
        )

    west, below = halo(w0)
    same, other = along_sy(message)
    lower = shifted(jnp.stack([same[:, :NEAR], other[:, :NEAR]]), "sx", -1)
    upper = shifted(jnp.stack([same[:, 2 * NEAR :], other[:, 2 * NEAR :]]), "sx", 1)
    numbers = jnp.concatenate([same[:, NEAR - 3], other[:, NEAR - 3]], 0).astype(jnp.int32)
    turned = kernel_call(
        pick_body,
        shape(half, block),
        (numbers, me, columns_all),
        2,
        scratch=(pltpu.VMEM((cases, cases), F32),),
        fast=(2,),
    )
    turned, west, below = lax.optimization_barrier((turned, west, below))
    given, back_east, back_north = give(w0, west, below)
    (kept,) = keep(given)
    rows_same, rows_other, (kept, lower, upper) = along_sy(turned, (kept, lower, upper))
    numbers = jnp.concatenate([rows_same[:, 0], rows_other[:, 0]], 0).astype(jnp.int32)
    own_part = kernel_call(
        functools.partial(near_body, gx),
        shape(gx * NEAR),
        (numbers, me, rows_same, rows_other),
        2,
        fast=(2, 3),
    )
    below_part = shifted(own_part, "sx", 1)
    beyond_part = shifted(own_part, "sx", -1)
    lanes = lax.dynamic_index_in_dim(jnp.asarray(lane_matrices(gy)), b % 2, 0, keepdims=False)

    send = kernel_call(
        first_coarse_body,
        shape(gx, ROWS),
        (lanes, own_part, same, other, lower, upper),
        fast=range(2, 6),
    )
    got = lax.all_to_all(send, "sx", 0, 0, tiled=True)
    u1, *w1, kappa, spare0, _, message = image_call(
        kept, back_east, back_north, got, edges, gain, w0, None, half
    )
    def coarse_solve(same, other):
        send = kernel_call(coarse_body, shape(gx, ROWS), (lanes, below_part, own_part, beyond_part, same, other), fast=(4, 5))
        return lax.all_to_all(send, "sx", 0, 0, tiled=True)

    west, below = halo(w1)
    same, other = along_sy(message)
    given, back_east, back_north = give(w1, west, below)
    got = coarse_solve(same, other)
    (kept,) = keep(given)
    u2, *w2, _, spare1, rows, message = image_call(
        kept, back_east, back_north, got, edges, gain, w1, kappa, half
    )
    west, below = halo(w2)
    same, other = along_sy(message)
    given, back_east, back_north = give(w2, west, below, True)
    same, given = lax.optimization_barrier((same, given))
    got = coarse_solve(same, other)
    kept, product = keep(given, True)
    last = kernel_call(sum_body, shape(gx * gy), (product, rows, got), fast=(0, 2))
    last = lax.all_to_all(last.reshape(gx * gy, 1, cases), ("sx", "sy"), 0, 0, tiled=True)
    u3, spare2 = kernel_call(
        functools.partial(image_body, True),
        (field, shape(8)),
        (kept, back_east, back_north, got, edges, gain),
        fast=range(4),
    )
    multipliers, residual = kernel_call(
        finish_body,
        (field, field),
        (
            kappa,
            spare0,
            spare1,
            spare2,
            last.reshape(gx * gy, cases),
            residual,
            *w0,
            *w1,
            *w2,
            u1,
            u2,
            u3,
        ),
        fast=(4,),
    )
    return multipliers.reshape(dual_rhs.shape), residual.reshape(dual_rhs.shape)


def solution(mesh):
    in_specs = (
        P("sx", "sy", None, None, None),
        P("sx", "sy", None, None),
        P("sx", "sy", None),
        P("sx", "sy", None),
        P("sx", "sy", None, None),
        P("sx", "sy", None, None),
        P("sx", "sy"),
    )
    out_specs = (P("sx", "sy", None, None, None), P("sx", "sy", None, None, None))
    return jax.shard_map(local, mesh=mesh, in_specs=in_specs, out_specs=out_specs, check_vma=False)
```

```python
import functools
import math

import numpy as np
import jax
import jax.numpy as jnp
from jax import lax
from jax.experimental import pallas as pl
from jax.experimental.pallas import tpu as pltpu
from jax.sharding import PartitionSpec as P

CS = 3
NEAR = 16
ROWS = 3 * NEAR
F32, BF16 = jnp.float32, jnp.bfloat16
SMEM = pl.BlockSpec(memory_space=pltpu.SMEM)


def shifted(array, axis, by):
    count = lax.axis_size(axis)
    return lax.ppermute(array, axis, [(i, (i + by) % count) for i in range(count)])


def along_sy(copies, beside=None):
    count = lax.axis_size("sy")
    groups = [[2 * z + core for z in range(count // 2)] for core in range(2)]
    same = lax.all_to_all(copies, "sy", 0, 0, tiled=True, axis_index_groups=groups)
    if beside is not None:
        same, beside = lax.optimization_barrier((same, beside))
    other = lax.ppermute(same, "sy", [(i, i ^ 1) for i in range(count)])
    return (same, other) if beside is None else (same, other, beside)


class Arriving:
    def __init__(self, source, held, arrived):
        self.copy = pltpu.make_async_copy(source, held, arrived)
        self.copy.start()
        self.held, self.shape, self.waiting = held, held.shape, True

    def settle(self):
        if self.waiting:
            self.copy.wait()
        self.waiting = False

    def __getitem__(self, index):
        self.settle()
        return self.held[index]


class Leaving:
    def __init__(self, held, target, arrived):
        self.copy = pltpu.make_async_copy(held, target, arrived)
        self.held, self.shape, self.sent = held, held.shape, False

    def __getitem__(self, index):
        return self.held[index]

    def __setitem__(self, index, value):
        self.held[index] = value

    def send(self):
        if not self.sent:
            self.copy.start()
        self.sent = True


def kernel_call(body, outs, operands, scalars=0, raw=(), scratch=(), fast=(), fast_outs=()):
    several = isinstance(outs, tuple)
    outs = outs if several else (outs,)
    operands = tuple(operands)
    count_in, count_out = len(operands), len(outs)
    slow_in = [k for k in range(scalars, count_in) if k not in fast]
    slow_out = [k for k in range(count_out) if k not in fast_outs]
    held = [pltpu.VMEM(operands[k].shape, operands[k].dtype) for k in slow_in]
    held += [pltpu.VMEM(outs[k].shape, outs[k].dtype) for k in slow_out]
    arrays = list(operands) + list(raw)
    moved = sum(4 * math.prod(array.shape) for array in arrays + list(outs))

    def wrapped(*refs):
        refs = list(refs)
        ins, refs = refs[: len(arrays)], refs[len(arrays) :]
        results, refs = refs[:count_out], refs[count_out:]
        buffers, refs = refs[: len(held)], refs[len(held) :]
        arrived, extra = refs[0], refs[1:]
        for n, k in enumerate(slow_in):
            ins[k] = Arriving(ins[k], buffers[n], arrived.at[n])
        for n, k in enumerate(slow_out, len(slow_in)):
            results[k] = Leaving(buffers[n], results[k], arrived.at[n])
        body(*ins, *results, *extra)
        for k in slow_in:
            ins[k].settle()
        for k in slow_out:
            results[k].send()
        for k in slow_out:
            results[k].copy.wait()

    def spec(k):
        return SMEM if k < scalars else pl.BlockSpec(memory_space=pltpu.VMEM if k in fast else pltpu.HBM)

    arrays = [
        array if k < scalars or k in fast else pltpu.with_memory_space_constraint(array, pltpu.HBM)
        for k, array in enumerate(arrays)
    ]
    out_specs = tuple(
        pl.BlockSpec(memory_space=pltpu.VMEM if k in fast_outs else pltpu.HBM) for k in range(count_out)
    )
    out_shape = tuple(
        (pltpu.VMEM if k in fast_outs else pltpu.HBM)(array.shape, array.dtype) for k, array in enumerate(outs)
    )
    got = pl.pallas_call(
        wrapped,
        in_specs=[spec(k) for k in range(len(arrays))],
        out_specs=out_specs,
        out_shape=out_shape,
        scratch_shapes=held + [pltpu.SemaphoreType.DMA((max(len(held), 1),))] + list(scratch),
        compiler_params=pltpu.CompilerParams(vmem_limit_bytes=16 * 2**20),
        cost_estimate=pl.CostEstimate(flops=4 * moved, bytes_accessed=moved, transcendentals=0),
    )(*arrays)
    return tuple(got) if several else got[0]


def split(value):
    high = value.astype(BF16)
    return high, (value - high.astype(F32)).astype(BF16)


def halves(value):
    return jnp.concatenate(split(value), 1)


def multiply(first, second):
    return jnp.dot(first, second, preferred_element_type=F32)


def place_matrices():
    place = [(0, 0), (-1, 0), (0, -1), (-1, -1)]
    out = np.zeros((4, ROWS, 32), np.float32)
    for s in range(2):
        for e in range(2):
            for k, (di, dj) in enumerate(place):
                for c in range(CS):
                    out[2 * s + e, (1 + di) * NEAR + (1 + s + dj) * CS + c, k * CS + c] += 1
                    row = (1 + di + (1 - e)) * NEAR + (1 + s + dj + e) * CS + c
                    out[2 * s + e, row, 16 + k * CS + c] -= 1
    return out


def lane_matrices(gy):
    out = np.zeros((2, 128, gy * NEAR), np.float32)
    for core in range(2):
        for slot in range(gy):
            z, other = slot % (gy // 2), slot // (gy // 2)
            source = 2 * z + (core ^ other)
            for jj in range(4):
                for c in range(CS):
                    j = (2 * source - 1 + jj) % (2 * gy)
                    out[core, j * CS + c, slot * NEAR + jj * CS + c] = 1
    return out


def message_to(out_ref, basis_ref, parts, extra):
    got = multiply(basis_ref[...], parts[...].reshape(basis_ref.shape[1], parts.shape[2]))
    cases = got.shape[1] // 2
    rows = got[:ROWS, :cases] + got[:ROWS, cases:] + got[ROWS:, :cases]
    index = lax.broadcasted_iota(jnp.int32, rows.shape, 0)
    for k, row in enumerate(extra):
        rows = jnp.where(index == NEAR - 4 + k, row, rows)
    for copy in range(out_ref.shape[0]):
        out_ref[copy] = rows
    return rows


def column_sum(value):
    return jnp.sum(value, axis=0, keepdims=True)


def wide_body(me, corner, coarse, out):
    block = coarse.shape[0]
    count = out.shape[0]
    lane = lax.broadcasted_iota(jnp.int32, (block, out.shape[2] - block), 1)
    spare = jnp.where(lane == 2 * me[0], corner[0, 0], 0) + jnp.where(lane == 2 * me[0] + 1, corner[1, 0], 0)
    wide = jnp.concatenate([coarse[...], spare.astype(F32)], 1)
    for copy in range(count):
        out[copy] = wide


def begin_body(count, corner, rhs, scaling, basis, east, above, places, coarse, blocks, *refs):
    res, east0, north0, north1, gain, edges, message, parts, tiles, moved = refs
    side, cases = rhs.shape[1], rhs.shape[2]
    copies = [
        pltpu.make_async_copy(blocks.at[4 * s, pl.ds(0, cases), pl.ds(0, cases)], tiles.at[s], moved.at[s])
        for s in range(2)
    ]
    for copy in copies:
        copy.start()
    high, low = split(scaling[...])
    least = (scaling[...] - high.astype(F32) - low.astype(F32)).astype(BF16)
    thirds = jnp.concatenate([high.astype(F32), low.astype(F32), least.astype(F32)], 0).astype(BF16)
    row = lax.broadcasted_iota(jnp.int32, (12, cases), 0)
    norm = jnp.zeros((1, cases), F32)
    for edge in range(4):
        s, e = divmod(edge, 2)
        index = lax.broadcasted_iota(jnp.int32, (side, cases), 0)
        mask = index < count[s, e]
        chosen = (row % 4 == edge).astype(F32).astype(BF16)
        wide = lax.dot_general(thirds, chosen, (((0,), (0,)), ((), ())), preferred_element_type=F32)
        gain[edge] = jnp.where(mask, wide, 0.0)
        res[edge] = jnp.where(mask, rhs[edge], 0.0)
        value = gain[edge] * res[edge]
        norm = norm + column_sum(res[edge] * value)
        put_edge(edge, value, east0, north0, north1, parts)
        own = basis[s, :, 2 * e * side : (2 * e + 1) * side].astype(BF16)
        if e == 0:
            other = east[s].astype(BF16)
        elif s == 0:
            other = basis[1, :, 3 * side :].astype(BF16)
        else:
            other = above[...].astype(BF16)
        place = places[edge].astype(BF16)
        value = multiply(place[:, : 4 * CS], own) + multiply(place[:, 16 : 16 + 4 * CS], other)
        high, low = split(value)
        edges[:ROWS, edge * side : (edge + 1) * side] = high
        edges[ROWS:, edge * side : (edge + 1) * side] = low
    for ref in (east0, north1, north0, res, gain, edges):
        ref.send()
    lane = lax.broadcasted_iota(jnp.int32, (1, cases), 1)
    numbers = jnp.where(lane == 0, corner[0, 0], 0) + jnp.where(lane == 1, corner[1, 0], 0)
    index = lax.broadcasted_iota(jnp.int32, (cases, cases), 0)
    diagonal = index == lax.broadcasted_iota(jnp.int32, (cases, cases), 1)
    size = jnp.zeros((1, cases), F32)
    for s in range(2):
        copies[s].wait()
        tile = tiles[s].astype(F32)
        size = size + jnp.sum(jnp.where(diagonal, tile, 0.0)) / (512.0 * cases)
    size = size + jnp.sum(jnp.abs(coarse[...])) / (16.0 * coarse.shape[0])
    message_to(message, edges, parts, [norm, numbers.astype(F32), size])


def put_edge(edge, value, east, north0, north1, parts):
    side = value.shape[0]
    if edge % 2 == 0:
        east[edge // 2] = value
    elif edge == 1:
        north0[...] = value
    else:
        north1[...] = value
    high, low = split(value)
    parts[edge, :, : value.shape[1]] = high
    parts[edge, :, value.shape[1] :] = low


def apply_rows(block, parts):
    out = multiply(block, parts)
    cases = out.shape[1] // 2
    return out[:, :cases] + out[:, cases:]


def fetch(source, held, arrived, wanted):
    copies = [pltpu.make_async_copy(source.at[k], held.at[n], arrived.at[n]) for n, k in enumerate(wanted)]
    for copy in copies:
        copy.start()
    return copies


def weighed(parts, s, q, out):
    side, cases = out.shape
    rows = parts[s, q * side : (q + 1) * side]
    return column_sum((rows[:, :cases].astype(F32) + rows[:, cases:].astype(F32)) * out)


GIVEN = (1, 5, 3)


def give_body(weigh, own_east, own_north0, own_north1, west, below, blocks, out_east, out_north, parts, *refs):
    *product, held, arrived = refs
    copies = fetch(blocks, held, arrived, GIVEN)
    side = west.shape[1]
    for s in range(2):
        parts[s, side : 2 * side] = halves(-west[s])
    parts[0, 3 * side :] = halves(-below[...])
    for s in range(2):
        parts[s, :side] = halves(own_east[s])
    parts[0, 2 * side : 3 * side] = halves(own_north0[...])
    parts[1, 3 * side :] = halves(-own_north0[...])
    parts[1, 2 * side : 3 * side] = halves(own_north1[...])
    total = 0.0
    for n, (s, q) in enumerate([(0, 1), (1, 1), (0, 3)]):
        copies[n].wait()
        value = apply_rows(held[n], parts[s])
        if n < 2:
            out_east[s] = value
        else:
            out_north[...] = value
        if n == 1:
            out_east.send()
        if weigh:
            total = total + weighed(parts, s, q, value)
    if weigh:
        product[0][...] = jnp.broadcast_to(total, product[0].shape)


def keep_body(weigh, parts, *refs):
    if weigh:
        product_in, blocks, out, product, held, arrived = refs
    else:
        blocks, out, held, arrived = refs
    copies = fetch(blocks, held, arrived, (0, 2, 7, 4, 6))
    total = 0.0
    for n, (edge, s, q) in enumerate([(0, 0, 0), (1, 0, 2), (1, 1, 3), (2, 1, 0), (3, 1, 2)]):
        copies[n].wait()
        value = apply_rows(held[n], parts[s])
        if weigh:
            total = total + weighed(parts, s, q, value)
        out[edge] = out[edge] - value if n == 2 else value
    if weigh:
        product[...] = jnp.broadcast_to(product_in[0:1] + total, product.shape)


def sum_body(product, rows, got, out):
    total = got[0]
    for k in range(1, got.shape[0]):
        total = total + got[k]
    index = lax.broadcasted_iota(jnp.int32, total.shape, 0) % NEAR
    value = product[0:1] + column_sum(jnp.where(index < 4 * CS, rows[...] * total, 0.0))
    out[...] = jnp.broadcast_to(value, out.shape)


def row_pieces(same, other, ii):
    return [ref[z, ii * NEAR : (ii + 1) * NEAR] for ref in (same, other) for z in range(same.shape[0])]


def lay_out(value, first, out):
    gx, cases = out.shape[0], out.shape[2]
    total = first[0][NEAR - 8 :]
    for piece in first[1:]:
        total = total + piece[NEAR - 8 :]
    index = lax.broadcasted_iota(jnp.int32, (8, cases), 0)
    for target in range(gx):
        for ii in range(3):
            at = ((target - 1 + ii) % gx) * NEAR
            out[target, ii * NEAR : ii * NEAR + 8] = value[at : at + 8]
            rest = value[at + 8 : at + 16]
            if ii == 0:
                rest = jnp.where(index < 4, rest, total)
            out[target, ii * NEAR + 8 : ii * NEAR + 16] = rest


def laid(source, lane):
    return tuple(multiply(part, lane).astype(BF16) for part in split(source[...]))


def coarse_body(lanes, below, own, beyond, same, other, out):
    cases = same.shape[2]
    lane = lanes[...].astype(BF16)
    value = 0.0
    for ii, source in enumerate((own, below, beyond)):
        gathered = halves(jnp.concatenate(row_pieces(same, other, (1, 0, 2)[ii]), 0))
        high, low = laid(source, lane)
        product = multiply(high, gathered)
        value = value + product[:, :cases] + product[:, cases:] + multiply(low, gathered[:, :cases])
    lay_out(value, row_pieces(same, other, 0), out)


def first_coarse_body(lanes, own, same, other, lower, upper, out):
    cases = same.shape[2]
    high, low = laid(own, lanes[...].astype(BF16))
    middle = row_pieces(same, other, 1)
    half = same.shape[0]
    pieces = [
        middle[k] + lower[k // half, k % half] + upper[k // half, k % half] for k in range(2 * half)
    ]
    gathered = halves(jnp.concatenate(pieces, 0))
    product = multiply(high, gathered)
    value = product[:, :cases] + product[:, cases:] + multiply(low, gathered[:, :cases])
    lay_out(value, row_pieces(same, other, 0), out)


def image_body(last, part, east, north, got, edges, gain, *refs):
    side, cases = part.shape[1], part.shape[2]
    if last:
        u_ref, spare = refs
    else:
        (prev_east, prev_north0, prev_north1), refs = refs[:3], refs[3:]
        kappa_in, refs = (refs[0], refs[1:]) if len(refs) == 10 else (None, refs)
        u_ref, w_east, w_north0, w_north1, kappa_out, spare, rows_out, message, own = refs
    total = got[0]
    for k in range(1, got.shape[0]):
        total = total + got[k]
    high, low = split(total)
    twice = jnp.concatenate(
        [jnp.concatenate([high, low], 1), jnp.concatenate([high, jnp.zeros_like(low)], 1)], 0
    )
    spare[...] = total[NEAR - 8 : NEAR]
    if not last:
        kappa = 4.0 / total[NEAR - 2 : NEAR - 1] if kappa_in is None else kappa_in[0:1]
        kappa_out[...] = jnp.broadcast_to(kappa, kappa_out.shape)
    first = jnp.zeros((1, cases), F32)
    second = jnp.zeros((1, cases), F32)
    for edge in (1, 3, 0, 2):
        coarse = lax.dot_general(
            edges[:, edge * side : (edge + 1) * side],
            twice,
            (((0,), (0,)), ((), ())),
            preferred_element_type=F32,
        )
        value = part[edge] + coarse[:, :cases] + coarse[:, cases:]
        if edge % 2 == 0:
            value = value - east[edge // 2]
        elif edge == 3:
            value = value - north[...]
        image = jnp.where(gain[edge] > 0.0, value, 0.0)
        u_ref[edge] = image
        if not last:
            previous = (prev_north0, prev_north1)[edge // 2][...] if edge % 2 else prev_east[edge // 2]
            first = first + column_sum(previous * image)
            following = kappa * gain[edge] * value
            second = second + column_sum(following * image)
            put_edge(edge, following, w_east, w_north0, w_north1, own)
    if last:
        return
    for ref in (w_east, w_north1, w_north0, u_ref):
        ref.send()
    rows_out[...] = message_to(message, edges, own, [first, second])


def image_call(part, east, north, got, edges, gain, previous, kappa, copies):
    _, side, cases = part.shape
    shape = lambda *dims: jax.ShapeDtypeStruct(dims + (cases,), F32)
    outs = (
        shape(4, side),
        shape(2, side),
        shape(side),
        shape(side),
        shape(8),
        shape(8),
        shape(ROWS),
        shape(copies, ROWS),
    )
    operands = (part, east, north, got, edges, gain, *previous) + (() if kappa is None else (kappa,))
    return kernel_call(
        functools.partial(image_body, False),
        outs,
        operands,
        scratch=(pltpu.VMEM((4, side, 2 * cases), BF16),),
        fast=range(4),
    )


def slot_of(source, core, half):
    return source // 2 + half * ((source + core) % 2)


def pick_body(numbers, me, columns, out, rows):
    half = numbers.shape[0] // 2
    block = out.shape[1]
    rows[...] = jnp.zeros_like(rows)
    core = me[1] % 2
    for j in range(4 * half):
        node = numbers[slot_of(j // 2, core, half), j % 2]
        for c in range(CS):
            at = node * CS + c
            rows[pl.ds(j * CS + c, 1)] = columns[pl.ds(at // block, 1), pl.ds(at % block, 1)].reshape(1, -1)
    turned = rows[...].T[:block]
    known = jnp.zeros((1, turned.shape[1]), F32)
    for k in range(columns.shape[0]):
        known = known + columns[k, :1]
    lane = lax.broadcasted_iota(jnp.int32, turned.shape, 1)
    turned = jnp.where(lane >= block, known, turned)
    for copy in range(half):
        out[copy] = turned


def near_body(gx, numbers, me, same, other, out):
    half = same.shape[0]
    block = same.shape[1]
    out[...] = jnp.zeros(out.shape, F32)
    core = me[1] % 2
    lane = lax.broadcasted_iota(jnp.int32, (1, same.shape[2]), 1)
    for jj in range(4):
        j = (2 * me[1] - 1 + jj + 4 * half) % (4 * half)
        slot = slot_of(j // 2, core, half)
        for i in range(gx):
            node = numbers[slot, block + 2 * i + j % 2]
            owner = node * CS // block
            row = node * CS - owner * block
            mine = owner % 2 == core
            for c in range(CS):
                first = same[pl.ds(owner // 2, 1), pl.ds(row + c, 1)].reshape(1, -1)
                second = other[pl.ds(owner // 2, 1), pl.ds(row + c, 1)].reshape(1, -1)
                value = jnp.where(mine, first, second)
                out[pl.ds(i * NEAR + jj * CS + c, 1)] = jnp.where(lane < block, value, 0.0)


def finish_body(kappa_ref, spare0, spare1, spare2, last, *refs):
    (res, *fields), (u1, u2, u3, mult_out, res_out) = refs[:10], refs[10:]
    kappa = kappa_ref[0:1]
    moments = [
        spare0[4:5],
        kappa * spare1[4:5],
        kappa * spare1[5:6],
        kappa * spare2[4:5],
        kappa * spare2[5:6],
        kappa * column_sum(last[...]),
    ]

    def form(first, second, shift):
        total = 0.0
        for i, x in enumerate(first):
            for j, y in enumerate(second):
                total = total + x * y * moments[i + j + shift]
        return total

    one = jnp.ones_like(kappa)
    rho, pi, gamma = [one], [one], []
    rz = moments[0]
    for iteration in range(3):
        step = rz / form(pi, pi, 1)
        gamma = [(gamma[k] if k < len(gamma) else 0.0) + step * pi[k] for k in range(len(pi))]
        rho = [one] + [-value for value in gamma]
        if iteration < 2:
            rz_new = form(rho, rho, 0)
            ratio = rz_new / rz
            pi = [rho[k] + (ratio * pi[k] if k < len(pi) else 0.0) for k in range(len(rho))]
            rz = rz_new
    gamma = [kappa * value for value in gamma]
    for edge in range(4):
        total = 0.0
        for k in range(3):
            east, north0, north1 = fields[3 * k : 3 * k + 3]
            value = east[edge // 2] if edge % 2 == 0 else (north0, north1)[edge // 2][...]
            total = total + gamma[k] * value
        mult_out[edge] = total
    mult_out.send()
    for edge in range(4):
        res_out[edge] = res[edge] - (gamma[0] * u1[edge] + gamma[1] * u2[edge] + gamma[2] * u3[edge])


def local(dual_rhs, scaling, dual_count, corner_map, local_ops, corner_basis, coarse_inverse):
    gx, gy = lax.axis_size("sx"), lax.axis_size("sy")
    a, b = lax.axis_index("sx"), lax.axis_index("sy")
    side, cases = dual_rhs.shape[3], dual_rhs.shape[4]
    rhs = dual_rhs.reshape(4, side, cases)
    blocks = local_ops.reshape(8, side, 4 * side)
    block = coarse_inverse.shape[0]
    half = gy // 2
    basis = corner_basis[0]
    me = jnp.stack([a, b]).astype(jnp.int32)
    shape = lambda *dims: jax.ShapeDtypeStruct(dims + (cases,), F32)
    field = shape(4, side)
    double = lambda *dims: jax.ShapeDtypeStruct(dims + (2 * cases,), BF16)
    wide = kernel_call(wide_body, shape(gx, block), (me, corner_map[0], coarse_inverse), 2)
    columns_all = lax.all_to_all(wide, "sx", 0, 0, tiled=True)
    wide_basis = basis.astype(F32)
    east = shifted(wide_basis[:, :, side : 2 * side], "sx", -1)
    above = shifted(wide_basis[0, :, 3 * side :], "sy", -1)

    residual, *w0, gain, edges, message = kernel_call(
        begin_body,
        (
            field,
            shape(2, side),
            shape(side),
            shape(side),
            field,
            jax.ShapeDtypeStruct((2 * ROWS, 4 * side), BF16),
            shape(half, ROWS),
        ),
        (
            dual_count[0],
            corner_map[0],
            rhs,
            scaling.reshape(4, side),
            wide_basis,
            east,
            above,
            jnp.asarray(place_matrices()),
            coarse_inverse,
        ),
        2,
        raw=(blocks,),
        scratch=(
            pltpu.VMEM((4, side, 2 * cases), BF16),
            pltpu.VMEM((2, cases, cases), BF16),
            pltpu.SemaphoreType.DMA((2,)),
        ),
        fast=(4, 5, 6),
    )
    message, columns_all = lax.optimization_barrier((message, columns_all))

    def halo(vector):
        return shifted(vector[0], "sx", 1), shifted(vector[2], "sy", 1)

    def held(count):
        return (pltpu.VMEM((count,) + blocks.shape[1:], BF16), pltpu.SemaphoreType.DMA((count,)))

    def give(own, west, below, weigh=False, near=(2, 3)):
        given_east, given_north, *given = kernel_call(
            functools.partial(give_body, weigh),
            (shape(2, side), shape(side), double(2, 4 * side)) + ((shape(8),) if weigh else ()),
            (*own, west, below),
            raw=(blocks,),
            scratch=held(3),
            fast=(3, 4),
            fast_outs=near,
        )
        return given, shifted(given_east, "sx", -1), shifted(given_north, "sy", -1)

    def keep(given, weigh=False, near=True):
        return kernel_call(
            functools.partial(keep_body, weigh),
            (field, shape(8)) if weigh else (field,),
            given,
            raw=(blocks,),
            scratch=held(5),
            fast=range(len(given) if near else 0),
            fast_outs=(0, 1),
        )

    west, below = halo(w0)
    same, other = along_sy(message)
    lower = shifted(jnp.stack([same[:, :NEAR], other[:, :NEAR]]), "sx", -1)
    upper = shifted(jnp.stack([same[:, 2 * NEAR :], other[:, 2 * NEAR :]]), "sx", 1)
    numbers = jnp.concatenate([same[:, NEAR - 3], other[:, NEAR - 3]], 0).astype(jnp.int32)
    turned = kernel_call(
        pick_body,
        shape(half, block),
        (numbers, me, columns_all),
        2,
        scratch=(pltpu.VMEM((cases, cases), F32),),
        fast=(2,),
    )
    turned, west, below = lax.optimization_barrier((turned, west, below))
    given, back_east, back_north = give(w0, west, below, near=())
    lanes = lax.dynamic_index_in_dim(jnp.asarray(lane_matrices(gy)), b % 2, 0, keepdims=False)
    rows_same, rows_other, (given, lower, upper, lanes) = along_sy(turned, (given, lower, upper, lanes))
    numbers = jnp.concatenate([rows_same[:, 0], rows_other[:, 0]], 0).astype(jnp.int32)
    own_part = kernel_call(
        functools.partial(near_body, gx),
        shape(gx * NEAR),
        (numbers, me, rows_same, rows_other),
        2,
        fast=(2, 3),
    )
    below_part = shifted(own_part, "sx", 1)
    beyond_part = shifted(own_part, "sx", -1)

    send = kernel_call(
        first_coarse_body,
        shape(gx, ROWS),
        (lanes, own_part, same, other, lower, upper),
        fast=range(2, 6),
    )
    send, given = lax.optimization_barrier((send, given))
    got = lax.all_to_all(send, "sx", 0, 0, tiled=True)
    (kept,) = keep(given, near=False)
    u1, *w1, kappa, spare0, _, message = image_call(
        kept, back_east, back_north, got, edges, gain, w0, None, half
    )
    def coarse_solve(same, other):
        send = kernel_call(coarse_body, shape(gx, ROWS), (lanes, below_part, own_part, beyond_part, same, other), fast=(4, 5))
        return lax.all_to_all(send, "sx", 0, 0, tiled=True)

    west, below = halo(w1)
    same, other, (below_part, beyond_part) = along_sy(message, (below_part, beyond_part))
    given, back_east, back_north = give(w1, west, below)
    got = coarse_solve(same, other)
    (kept,) = keep(given)
    u2, *w2, _, spare1, rows, message = image_call(
        kept, back_east, back_north, got, edges, gain, w1, kappa, half
    )
    west, below = halo(w2)
    same, other = along_sy(message)
    given, back_east, back_north = give(w2, west, below, True)
    same, given = lax.optimization_barrier((same, given))
    got = coarse_solve(same, other)
    kept, product = keep(given, True)
    last = kernel_call(sum_body, shape(gx * gy), (product, rows, got), fast=(0, 2))
    last = lax.all_to_all(last.reshape(gx * gy, 1, cases), ("sx", "sy"), 0, 0, tiled=True)
    u3, spare2 = kernel_call(
        functools.partial(image_body, True),
        (field, shape(8)),
        (kept, back_east, back_north, got, edges, gain),
        fast=range(4),
    )
    multipliers, residual = kernel_call(
        finish_body,
        (field, field),
        (
            kappa,
            spare0,
            spare1,
            spare2,
            last.reshape(gx * gy, cases),
            residual,
            *w0,
            *w1,
            *w2,
            u1,
            u2,
            u3,
        ),
        fast=(4,),
    )
    return multipliers.reshape(dual_rhs.shape), residual.reshape(dual_rhs.shape)


def solution(mesh):
    in_specs = (
        P("sx", "sy", None, None, None),
        P("sx", "sy", None, None),
        P("sx", "sy", None),
        P("sx", "sy", None),
        P("sx", "sy", None, None),
        P("sx", "sy", None, None),
        P("sx", "sy"),
    )
    out_specs = (P("sx", "sy", None, None, None), P("sx", "sy", None, None, None))
    return jax.shard_map(local, mesh=mesh, in_specs=in_specs, out_specs=out_specs, check_vma=False)
```

```python
import functools
import math

import numpy as np
import jax
import jax.numpy as jnp
from jax import lax
from jax.experimental import pallas as pl
from jax.experimental.pallas import tpu as pltpu
from jax.sharding import PartitionSpec as P

CS = 3
NEAR = 16
ROWS = 3 * NEAR
F32, BF16 = jnp.float32, jnp.bfloat16
SMEM = pl.BlockSpec(memory_space=pltpu.SMEM)


def shifted(array, axis, by):
    count = lax.axis_size(axis)
    return lax.ppermute(array, axis, [(i, (i + by) % count) for i in range(count)])


def along_sy(copies, beside=None):
    count = lax.axis_size("sy")
    groups = [[2 * z + core for z in range(count // 2)] for core in range(2)]
    same = lax.all_to_all(copies, "sy", 0, 0, tiled=True, axis_index_groups=groups)
    if beside is not None:
        same, beside = lax.optimization_barrier((same, beside))
    other = lax.ppermute(same, "sy", [(i, i ^ 1) for i in range(count)])
    return (same, other) if beside is None else (same, other, beside)


class Arriving:
    def __init__(self, source, held, arrived):
        self.copy = pltpu.make_async_copy(source, held, arrived)
        self.copy.start()
        self.held, self.shape, self.waiting = held, held.shape, True

    def settle(self):
        if self.waiting:
            self.copy.wait()
        self.waiting = False

    def __getitem__(self, index):
        self.settle()
        return self.held[index]


class Leaving:
    def __init__(self, held, target, arrived):
        self.copy = pltpu.make_async_copy(held, target, arrived)
        self.held, self.shape, self.sent = held, held.shape, False

    def __getitem__(self, index):
        return self.held[index]

    def __setitem__(self, index, value):
        self.held[index] = value

    def send(self):
        if not self.sent:
            self.copy.start()
        self.sent = True


def kernel_call(body, outs, operands, scalars=0, raw=(), scratch=(), fast=(), fast_outs=()):
    several = isinstance(outs, tuple)
    outs = outs if several else (outs,)
    operands = tuple(operands)
    count_in, count_out = len(operands), len(outs)
    slow_in = [k for k in range(scalars, count_in) if k not in fast]
    slow_out = [k for k in range(count_out) if k not in fast_outs]
    held = [pltpu.VMEM(operands[k].shape, operands[k].dtype) for k in slow_in]
    held += [pltpu.VMEM(outs[k].shape, outs[k].dtype) for k in slow_out]
    arrays = list(operands) + list(raw)
    moved = sum(4 * math.prod(array.shape) for array in arrays + list(outs))

    def wrapped(*refs):
        refs = list(refs)
        ins, refs = refs[: len(arrays)], refs[len(arrays) :]
        results, refs = refs[:count_out], refs[count_out:]
        buffers, refs = refs[: len(held)], refs[len(held) :]
        arrived, extra = refs[0], refs[1:]
        for n, k in enumerate(slow_in):
            ins[k] = Arriving(ins[k], buffers[n], arrived.at[n])
        for n, k in enumerate(slow_out, len(slow_in)):
            results[k] = Leaving(buffers[n], results[k], arrived.at[n])
        body(*ins, *results, *extra)
        for k in slow_in:
            ins[k].settle()
        for k in slow_out:
            results[k].send()
        for k in slow_out:
            results[k].copy.wait()

    def spec(k):
        return SMEM if k < scalars else pl.BlockSpec(memory_space=pltpu.VMEM if k in fast else pltpu.HBM)

    arrays = [
        array if k < scalars or k in fast else pltpu.with_memory_space_constraint(array, pltpu.HBM)
        for k, array in enumerate(arrays)
    ]
    out_specs = tuple(
        pl.BlockSpec(memory_space=pltpu.VMEM if k in fast_outs else pltpu.HBM) for k in range(count_out)
    )
    out_shape = tuple(
        (pltpu.VMEM if k in fast_outs else pltpu.HBM)(array.shape, array.dtype) for k, array in enumerate(outs)
    )
    got = pl.pallas_call(
        wrapped,
        in_specs=[spec(k) for k in range(len(arrays))],
        out_specs=out_specs,
        out_shape=out_shape,
        scratch_shapes=held + [pltpu.SemaphoreType.DMA((max(len(held), 1),))] + list(scratch),
        compiler_params=pltpu.CompilerParams(vmem_limit_bytes=16 * 2**20),
        cost_estimate=pl.CostEstimate(flops=4 * moved, bytes_accessed=moved, transcendentals=0),
    )(*arrays)
    return tuple(got) if several else got[0]


def split(value):
    high = value.astype(BF16)
    return high, (value - high.astype(F32)).astype(BF16)


def halves(value):
    return jnp.concatenate(split(value), 1)


def multiply(first, second):
    return jnp.dot(first, second, preferred_element_type=F32)


def place_matrices():
    place = [(0, 0), (-1, 0), (0, -1), (-1, -1)]
    out = np.zeros((4, ROWS, 32), np.float32)
    for s in range(2):
        for e in range(2):
            for k, (di, dj) in enumerate(place):
                for c in range(CS):
                    out[2 * s + e, (1 + di) * NEAR + (1 + s + dj) * CS + c, k * CS + c] += 1
                    row = (1 + di + (1 - e)) * NEAR + (1 + s + dj + e) * CS + c
                    out[2 * s + e, row, 16 + k * CS + c] -= 1
    return out


def lane_matrices(gy):
    out = np.zeros((2, 128, gy * NEAR), np.float32)
    for core in range(2):
        for slot in range(gy):
            z, other = slot % (gy // 2), slot // (gy // 2)
            source = 2 * z + (core ^ other)
            for jj in range(4):
                for c in range(CS):
                    j = (2 * source - 1 + jj) % (2 * gy)
                    out[core, j * CS + c, slot * NEAR + jj * CS + c] = 1
    return out


def message_to(out_ref, basis_ref, parts, extra):
    got = multiply(basis_ref[...], parts[...].reshape(basis_ref.shape[1], parts.shape[2]))
    cases = got.shape[1] // 2
    rows = got[:ROWS, :cases] + got[:ROWS, cases:] + got[ROWS:, :cases]
    index = lax.broadcasted_iota(jnp.int32, rows.shape, 0)
    for k, row in enumerate(extra):
        rows = jnp.where(index == NEAR - 4 + k, row, rows)
    for copy in range(out_ref.shape[0]):
        out_ref[copy] = rows
    return rows


def column_sum(value):
    return jnp.sum(value, axis=0, keepdims=True)


def wide_body(me, corner, coarse, out):
    block = coarse.shape[0]
    count = out.shape[0]
    lane = lax.broadcasted_iota(jnp.int32, (block, out.shape[2] - block), 1)
    spare = jnp.where(lane == 2 * me[0], corner[0, 0], 0) + jnp.where(lane == 2 * me[0] + 1, corner[1, 0], 0)
    wide = jnp.concatenate([coarse[...], spare.astype(F32)], 1)
    for copy in range(count):
        out[copy] = wide


def begin_body(count, corner, rhs, scaling, basis, east, above, places, coarse, blocks, *refs):
    res, east0, north0, north1, gain, edges, message, parts, tiles, moved = refs
    side, cases = rhs.shape[1], rhs.shape[2]
    copies = [
        pltpu.make_async_copy(blocks.at[4 * s, pl.ds(0, cases), pl.ds(0, cases)], tiles.at[s], moved.at[s])
        for s in range(2)
    ]
    for copy in copies:
        copy.start()
    high, low = split(scaling[...])
    least = (scaling[...] - high.astype(F32) - low.astype(F32)).astype(BF16)
    thirds = jnp.concatenate([high.astype(F32), low.astype(F32), least.astype(F32)], 0).astype(BF16)
    row = lax.broadcasted_iota(jnp.int32, (12, cases), 0)
    norm = jnp.zeros((1, cases), F32)
    for edge in range(4):
        s, e = divmod(edge, 2)
        index = lax.broadcasted_iota(jnp.int32, (side, cases), 0)
        mask = index < count[s, e]
        chosen = (row % 4 == edge).astype(F32).astype(BF16)
        wide = lax.dot_general(thirds, chosen, (((0,), (0,)), ((), ())), preferred_element_type=F32)
        gain[edge] = jnp.where(mask, wide, 0.0)
        res[edge] = jnp.where(mask, rhs[edge], 0.0)
        value = gain[edge] * res[edge]
        norm = norm + column_sum(res[edge] * value)
        put_edge(edge, value, east0, north0, north1, parts)
        own = basis[s, :, 2 * e * side : (2 * e + 1) * side].astype(BF16)
        if e == 0:
            other = east[s].astype(BF16)
        elif s == 0:
            other = basis[1, :, 3 * side :].astype(BF16)
        else:
            other = above[...].astype(BF16)
        place = places[edge].astype(BF16)
        value = multiply(place[:, : 4 * CS], own) + multiply(place[:, 16 : 16 + 4 * CS], other)
        high, low = split(value)
        edges[:ROWS, edge * side : (edge + 1) * side] = high
        edges[ROWS:, edge * side : (edge + 1) * side] = low
    for ref in (east0, north1, north0, res, gain, edges):
        ref.send()
    lane = lax.broadcasted_iota(jnp.int32, (1, cases), 1)
    numbers = jnp.where(lane == 0, corner[0, 0], 0) + jnp.where(lane == 1, corner[1, 0], 0)
    index = lax.broadcasted_iota(jnp.int32, (cases, cases), 0)
    diagonal = index == lax.broadcasted_iota(jnp.int32, (cases, cases), 1)
    size = jnp.zeros((1, cases), F32)
    for s in range(2):
        copies[s].wait()
        tile = tiles[s].astype(F32)
        size = size + jnp.sum(jnp.where(diagonal, tile, 0.0)) / (512.0 * cases)
    size = size + jnp.sum(jnp.abs(coarse[...])) / (16.0 * coarse.shape[0])
    message_to(message, edges, parts, [norm, numbers.astype(F32), size])


def put_edge(edge, value, east, north0, north1, parts):
    side = value.shape[0]
    if edge % 2 == 0:
        east[edge // 2] = value
    elif edge == 1:
        north0[...] = value
    else:
        north1[...] = value
    high, low = split(value)
    parts[edge, :, : value.shape[1]] = high
    parts[edge, :, value.shape[1] :] = low


def apply_rows(block, parts):
    out = multiply(block, parts)
    cases = out.shape[1] // 2
    return out[:, :cases] + out[:, cases:]


def fetch(source, held, arrived, wanted):
    copies = [pltpu.make_async_copy(source.at[k], held.at[n], arrived.at[n]) for n, k in enumerate(wanted)]
    for copy in copies:
        copy.start()
    return copies


def weighed(parts, s, q, out):
    side, cases = out.shape
    rows = parts[s, q * side : (q + 1) * side]
    return column_sum((rows[:, :cases].astype(F32) + rows[:, cases:].astype(F32)) * out)


GIVEN = (1, 5, 3)


def give_body(weigh, own_east, own_north0, own_north1, west, below, blocks, out_east, out_north, parts, *refs):
    *product, held, arrived = refs
    copies = fetch(blocks, held, arrived, GIVEN)
    side = west.shape[1]
    for s in range(2):
        parts[s, side : 2 * side] = halves(-west[s])
    parts[0, 3 * side :] = halves(-below[...])
    for s in range(2):
        parts[s, :side] = halves(own_east[s])
    parts[0, 2 * side : 3 * side] = halves(own_north0[...])
    parts[1, 3 * side :] = halves(-own_north0[...])
    parts[1, 2 * side : 3 * side] = halves(own_north1[...])
    total = 0.0
    for n, (s, q) in enumerate([(0, 1), (1, 1), (0, 3)]):
        copies[n].wait()
        value = apply_rows(held[n], parts[s])
        if n < 2:
            out_east[s] = value
        else:
            out_north[...] = value
        if n == 1:
            out_east.send()
        if weigh:
            total = total + weighed(parts, s, q, value)
    if weigh:
        product[0][...] = jnp.broadcast_to(total, product[0].shape)


def keep_body(weigh, parts, *refs):
    if weigh:
        product_in, blocks, out, product, held, arrived = refs
    else:
        blocks, out, held, arrived = refs
    copies = fetch(blocks, held, arrived, (0, 2, 7, 4, 6))
    total = 0.0
    for n, (edge, s, q) in enumerate([(0, 0, 0), (1, 0, 2), (1, 1, 3), (2, 1, 0), (3, 1, 2)]):
        copies[n].wait()
        value = apply_rows(held[n], parts[s])
        if weigh:
            total = total + weighed(parts, s, q, value)
        out[edge] = out[edge] - value if n == 2 else value
    if weigh:
        product[...] = jnp.broadcast_to(product_in[0:1] + total, product.shape)


def sum_body(product, rows, got, out):
    total = got[0]
    for k in range(1, got.shape[0]):
        total = total + got[k]
    index = lax.broadcasted_iota(jnp.int32, total.shape, 0) % NEAR
    value = product[0:1] + column_sum(jnp.where(index < 4 * CS, rows[...] * total, 0.0))
    out[...] = jnp.broadcast_to(value, out.shape)


def row_pieces(same, other, ii):
    return [ref[z, ii * NEAR : (ii + 1) * NEAR] for ref in (same, other) for z in range(same.shape[0])]


def lay_out(value, first, out):
    gx, cases = out.shape[0], out.shape[2]
    total = first[0][NEAR - 8 :]
    for piece in first[1:]:
        total = total + piece[NEAR - 8 :]
    index = lax.broadcasted_iota(jnp.int32, (8, cases), 0)
    for target in range(gx):
        for ii in range(3):
            at = ((target - 1 + ii) % gx) * NEAR
            out[target, ii * NEAR : ii * NEAR + 8] = value[at : at + 8]
            rest = value[at + 8 : at + 16]
            if ii == 0:
                rest = jnp.where(index < 4, rest, total)
            out[target, ii * NEAR + 8 : ii * NEAR + 16] = rest


def laid(source, lane):
    return tuple(multiply(part, lane).astype(BF16) for part in split(source[...]))


def coarse_body(lanes, below, own, beyond, same, other, out):
    cases = same.shape[2]
    lane = lanes[...].astype(BF16)
    value = 0.0
    for ii, source in enumerate((own, below, beyond)):
        gathered = halves(jnp.concatenate(row_pieces(same, other, (1, 0, 2)[ii]), 0))
        high, low = laid(source, lane)
        product = multiply(high, gathered)
        value = value + product[:, :cases] + product[:, cases:] + multiply(low, gathered[:, :cases])
    lay_out(value, row_pieces(same, other, 0), out)


def first_coarse_body(lanes, own, same, other, lower, upper, out):
    cases = same.shape[2]
    high, low = laid(own, lanes[...].astype(BF16))
    middle = row_pieces(same, other, 1)
    half = same.shape[0]
    pieces = [
        middle[k] + lower[k // half, k % half] + upper[k // half, k % half] for k in range(2 * half)
    ]
    gathered = halves(jnp.concatenate(pieces, 0))
    product = multiply(high, gathered)
    value = product[:, :cases] + product[:, cases:] + multiply(low, gathered[:, :cases])
    lay_out(value, row_pieces(same, other, 0), out)


def image_body(last, part, east, north, got, edges, gain, *refs):
    side, cases = part.shape[1], part.shape[2]
    if last:
        u_ref, spare = refs
    else:
        (prev_east, prev_north0, prev_north1), refs = refs[:3], refs[3:]
        kappa_in, refs = (refs[0], refs[1:]) if len(refs) == 10 else (None, refs)
        u_ref, w_east, w_north0, w_north1, kappa_out, spare, rows_out, message, own = refs
    total = got[0]
    for k in range(1, got.shape[0]):
        total = total + got[k]
    high, low = split(total)
    twice = jnp.concatenate(
        [jnp.concatenate([high, low], 1), jnp.concatenate([high, jnp.zeros_like(low)], 1)], 0
    )
    spare[...] = total[NEAR - 8 : NEAR]
    if not last:
        kappa = 4.0 / total[NEAR - 2 : NEAR - 1] if kappa_in is None else kappa_in[0:1]
        kappa_out[...] = jnp.broadcast_to(kappa, kappa_out.shape)
    first = jnp.zeros((1, cases), F32)
    second = jnp.zeros((1, cases), F32)
    for edge in (1, 3, 0, 2):
        coarse = lax.dot_general(
            edges[:, edge * side : (edge + 1) * side],
            twice,
            (((0,), (0,)), ((), ())),
            preferred_element_type=F32,
        )
        value = part[edge] + coarse[:, :cases] + coarse[:, cases:]
        if edge % 2 == 0:
            value = value - east[edge // 2]
        elif edge == 3:
            value = value - north[...]
        image = jnp.where(gain[edge] > 0.0, value, 0.0)
        u_ref[edge] = image
        if not last:
            previous = (prev_north0, prev_north1)[edge // 2][...] if edge % 2 else prev_east[edge // 2]
            first = first + column_sum(previous * image)
            following = kappa * gain[edge] * value
            second = second + column_sum(following * image)
            put_edge(edge, following, w_east, w_north0, w_north1, own)
    if last:
        return
    for ref in (w_east, w_north1, w_north0, u_ref):
        ref.send()
    rows_out[...] = message_to(message, edges, own, [first, second])


def image_call(part, east, north, got, edges, gain, previous, kappa, copies):
    _, side, cases = part.shape
    shape = lambda *dims: jax.ShapeDtypeStruct(dims + (cases,), F32)
    outs = (
        shape(4, side),
        shape(2, side),
        shape(side),
        shape(side),
        shape(8),
        shape(8),
        shape(ROWS),
        shape(copies, ROWS),
    )
    operands = (part, east, north, got, edges, gain, *previous) + (() if kappa is None else (kappa,))
    return kernel_call(
        functools.partial(image_body, False),
        outs,
        operands,
        scratch=(pltpu.VMEM((4, side, 2 * cases), BF16),),
        fast=range(4),
    )


def slot_of(source, core, half):
    return source // 2 + half * ((source + core) % 2)


def pick_body(numbers, me, columns, out, rows):
    half = numbers.shape[0] // 2
    block = out.shape[1]
    rows[...] = jnp.zeros_like(rows)
    core = me[1] % 2
    for j in range(4 * half):
        node = numbers[slot_of(j // 2, core, half), j % 2]
        for c in range(CS):
            at = node * CS + c
            rows[pl.ds(j * CS + c, 1)] = columns[pl.ds(at // block, 1), pl.ds(at % block, 1)].reshape(1, -1)
    turned = rows[...].T[:block]
    known = jnp.zeros((1, turned.shape[1]), F32)
    for k in range(columns.shape[0]):
        known = known + columns[k, :1]
    lane = lax.broadcasted_iota(jnp.int32, turned.shape, 1)
    turned = jnp.where(lane >= block, known, turned)
    for copy in range(half):
        out[copy] = turned


def near_body(gx, numbers, me, same, other, out):
    half = same.shape[0]
    block = same.shape[1]
    out[...] = jnp.zeros(out.shape, F32)
    core = me[1] % 2
    lane = lax.broadcasted_iota(jnp.int32, (1, same.shape[2]), 1)
    for jj in range(4):
        j = (2 * me[1] - 1 + jj + 4 * half) % (4 * half)
        slot = slot_of(j // 2, core, half)
        for i in range(gx):
            node = numbers[slot, block + 2 * i + j % 2]
            owner = node * CS // block
            row = node * CS - owner * block
            mine = owner % 2 == core
            for c in range(CS):
                first = same[pl.ds(owner // 2, 1), pl.ds(row + c, 1)].reshape(1, -1)
                second = other[pl.ds(owner // 2, 1), pl.ds(row + c, 1)].reshape(1, -1)
                value = jnp.where(mine, first, second)
                out[pl.ds(i * NEAR + jj * CS + c, 1)] = jnp.where(lane < block, value, 0.0)


def finish_body(kappa_ref, spare0, spare1, spare2, last, *refs):
    (res, *fields), (u1, u2, u3, mult_out, res_out) = refs[:10], refs[10:]
    kappa = kappa_ref[0:1]
    moments = [
        spare0[4:5],
        kappa * spare1[4:5],
        kappa * spare1[5:6],
        kappa * spare2[4:5],
        kappa * spare2[5:6],
        kappa * column_sum(last[...]),
    ]

    def form(first, second, shift):
        total = 0.0
        for i, x in enumerate(first):
            for j, y in enumerate(second):
                total = total + x * y * moments[i + j + shift]
        return total

    one = jnp.ones_like(kappa)
    rho, pi, gamma = [one], [one], []
    rz = moments[0]
    for iteration in range(3):
        step = rz / form(pi, pi, 1)
        gamma = [(gamma[k] if k < len(gamma) else 0.0) + step * pi[k] for k in range(len(pi))]
        rho = [one] + [-value for value in gamma]
        if iteration < 2:
            rz_new = form(rho, rho, 0)
            ratio = rz_new / rz
            pi = [rho[k] + (ratio * pi[k] if k < len(pi) else 0.0) for k in range(len(rho))]
            rz = rz_new
    gamma = [kappa * value for value in gamma]
    for edge in range(4):
        total = 0.0
        for k in range(3):
            east, north0, north1 = fields[3 * k : 3 * k + 3]
            value = east[edge // 2] if edge % 2 == 0 else (north0, north1)[edge // 2][...]
            total = total + gamma[k] * value
        mult_out[edge] = total
    mult_out.send()
    for edge in range(4):
        res_out[edge] = res[edge] - (gamma[0] * u1[edge] + gamma[1] * u2[edge] + gamma[2] * u3[edge])


def local(dual_rhs, scaling, dual_count, corner_map, local_ops, corner_basis, coarse_inverse):
    gx, gy = lax.axis_size("sx"), lax.axis_size("sy")
    a, b = lax.axis_index("sx"), lax.axis_index("sy")
    side, cases = dual_rhs.shape[3], dual_rhs.shape[4]
    rhs = dual_rhs.reshape(4, side, cases)
    blocks = local_ops.reshape(8, side, 4 * side)
    block = coarse_inverse.shape[0]
    half = gy // 2
    basis = corner_basis[0]
    me = jnp.stack([a, b]).astype(jnp.int32)
    shape = lambda *dims: jax.ShapeDtypeStruct(dims + (cases,), F32)
    field = shape(4, side)
    double = lambda *dims: jax.ShapeDtypeStruct(dims + (2 * cases,), BF16)
    wide = kernel_call(wide_body, shape(gx, block), (me, corner_map[0], coarse_inverse), 2)
    columns_all = lax.all_to_all(wide, "sx", 0, 0, tiled=True)
    wide_basis = basis.astype(F32)
    east = shifted(wide_basis[:, :, side : 2 * side], "sx", -1)
    above = shifted(wide_basis[0, :, 3 * side :], "sy", -1)

    residual, *w0, gain, edges, message = kernel_call(
        begin_body,
        (
            field,
            shape(2, side),
            shape(side),
            shape(side),
            field,
            jax.ShapeDtypeStruct((2 * ROWS, 4 * side), BF16),
            shape(half, ROWS),
        ),
        (
            dual_count[0],
            corner_map[0],
            rhs,
            scaling.reshape(4, side),
            wide_basis,
            east,
            above,
            jnp.asarray(place_matrices()),
            coarse_inverse,
        ),
        2,
        raw=(blocks,),
        scratch=(
            pltpu.VMEM((4, side, 2 * cases), BF16),
            pltpu.VMEM((2, cases, cases), BF16),
            pltpu.SemaphoreType.DMA((2,)),
        ),
        fast=(4, 5, 6),
    )
    message, columns_all = lax.optimization_barrier((message, columns_all))

    def halo(vector):
        return shifted(vector[0], "sx", 1), shifted(vector[2], "sy", 1)

    def held(count):
        return (pltpu.VMEM((count,) + blocks.shape[1:], BF16), pltpu.SemaphoreType.DMA((count,)))

    def give(own, west, below, weigh=False, near=(2, 3)):
        given_east, given_north, *given = kernel_call(
            functools.partial(give_body, weigh),
            (shape(2, side), shape(side), double(2, 4 * side)) + ((shape(8),) if weigh else ()),
            (*own, west, below),
            raw=(blocks,),
            scratch=held(3),
            fast=(3, 4),
            fast_outs=near,
        )
        return given, shifted(given_east, "sx", -1), shifted(given_north, "sy", -1)

    def keep(given, weigh=False, near=True):
        return kernel_call(
            functools.partial(keep_body, weigh),
            (field, shape(8)) if weigh else (field,),
            given,
            raw=(blocks,),
            scratch=held(5),
            fast=range(len(given) if near else 0),
            fast_outs=(0, 1),
        )

    west, below = halo(w0)
    same, other = along_sy(message)
    lower = shifted(jnp.stack([same[:, :NEAR], other[:, :NEAR]]), "sx", -1)
    upper = shifted(jnp.stack([same[:, 2 * NEAR :], other[:, 2 * NEAR :]]), "sx", 1)
    numbers = jnp.concatenate([same[:, NEAR - 3], other[:, NEAR - 3]], 0).astype(jnp.int32)
    turned = kernel_call(
        pick_body,
        shape(half, block),
        (numbers, me, columns_all),
        2,
        scratch=(pltpu.VMEM((cases, cases), F32),),
        fast=(2,),
    )
    turned, west, below = lax.optimization_barrier((turned, west, below))
    given, back_east, back_north = give(w0, west, below, near=())
    lanes = lax.dynamic_index_in_dim(jnp.asarray(lane_matrices(gy)), b % 2, 0, keepdims=False)
    rows_same, rows_other, (given, lower, upper, lanes) = along_sy(turned, (given, lower, upper, lanes))
    numbers = jnp.concatenate([rows_same[:, 0], rows_other[:, 0]], 0).astype(jnp.int32)
    own_part = kernel_call(
        functools.partial(near_body, gx),
        shape(gx * NEAR),
        (numbers, me, rows_same, rows_other),
        2,
        fast=(2, 3),
    )
    below_part = shifted(own_part, "sx", 1)
    beyond_part = shifted(own_part, "sx", -1)

    send = kernel_call(
        first_coarse_body,
        shape(gx, ROWS),
        (lanes, own_part, same, other, lower, upper),
        fast=range(2, 6),
    )
    send, given = lax.optimization_barrier((send, given))
    got = lax.all_to_all(send, "sx", 0, 0, tiled=True)
    (kept,) = keep(given, near=False)
    u1, *w1, kappa, spare0, _, message = image_call(
        kept, back_east, back_north, got, edges, gain, w0, None, half
    )
    def coarse_solve(same, other):
        send = kernel_call(coarse_body, shape(gx, ROWS), (lanes, below_part, own_part, beyond_part, same, other), fast=(4, 5))
        return lax.all_to_all(send, "sx", 0, 0, tiled=True)

    west, below = halo(w1)
    same, other = along_sy(message)
    given, back_east, back_north = give(w1, west, below)
    got = coarse_solve(same, other)
    (kept,) = keep(given)
    u2, *w2, _, spare1, rows, message = image_call(
        kept, back_east, back_north, got, edges, gain, w1, kappa, half
    )
    west, below = halo(w2)
    same, other = along_sy(message)
    given, back_east, back_north = give(w2, west, below, True)
    same, given = lax.optimization_barrier((same, given))
    got = coarse_solve(same, other)
    kept, product = keep(given, True)
    last = kernel_call(sum_body, shape(gx * gy), (product, rows, got), fast=(0, 2))
    last = lax.all_to_all(last.reshape(gx * gy, 1, cases), ("sx", "sy"), 0, 0, tiled=True)
    u3, spare2 = kernel_call(
        functools.partial(image_body, True),
        (field, shape(8)),
        (kept, back_east, back_north, got, edges, gain),
        fast=range(4),
    )
    multipliers, residual = kernel_call(
        finish_body,
        (field, field),
        (
            kappa,
            spare0,
            spare1,
            spare2,
            last.reshape(gx * gy, cases),
            residual,
            *w0,
            *w1,
            *w2,
            u1,
            u2,
            u3,
        ),
        fast=(4,),
    )
    return multipliers.reshape(dual_rhs.shape), residual.reshape(dual_rhs.shape)


def solution(mesh):
    in_specs = (
        P("sx", "sy", None, None, None),
        P("sx", "sy", None, None),
        P("sx", "sy", None),
        P("sx", "sy", None),
        P("sx", "sy", None, None),
        P("sx", "sy", None, None),
        P("sx", "sy"),
    )
    out_specs = (P("sx", "sy", None, None, None), P("sx", "sy", None, None, None))
    return jax.shard_map(local, mesh=mesh, in_specs=in_specs, out_specs=out_specs, check_vma=False)
```
